256 devices in a mesh: row: 32 (over x, z_hi, core), feat: 8 (over y, z_lo).
Axes of the slice: x: 4, y: 4, z: 8 (z_hi: 4, z_lo: 2; z = z_hi * 2 + z_lo), core: 2. Of those that a mesh axis runs over, the one named last changes fastest.
Arguments:
- features: bfloat16 [8192, 7168], P('row', 'feat'), may hold values from -6 to 6
- weights: float32 [7168], P('feat'), may hold values from -0.0625 to 0.0625
- labels: int32 [8192], P('row'), may hold values 0 or 1
- sign_bits: int32 [8192], P('row'), may hold values 0 or 1
- sample_rows: int32 [7680], P('row'), may hold values from 0 to 255, as said below
Outputs:
- gram: float32 [7168, 7168], P('row', 'feat')
- gradient: float32 [7168], P('feat')
The draws below stay inside these ranges and needn't reach their ends.
Inputs may be any that keep to these rules, and one draw needn't show every extreme that they name: `sample_rows`: each block of 240 entries is strictly rising, starts at 0 and ends at 255.
All inputs are finite; a program needn't handle non-finite values. No bound on the sum of `labels` or of `sign_bits` on one device may be relied on, other than what follows from the above.
Results may differ from the reference program's by a relative error of at most 0.0028.
Values may be sent and summed in bfloat16 or wider, within the bound.
A program may use at most 128 MiB of HBM per device.

```python
import jax
import jax.numpy as jnp
from jax import lax

D = 7168
ROWS_DEV = 256
SKETCH_DEV = 240
ROWS = 8192
SKETCH = 7680
N_ROW = 32


def draw_sample_rows(key, part):
    key = jax.random.fold_in(key, 11)
    blocks = SKETCH // SKETCH_DEV
    inner = ROWS_DEV - 2
    scores = jax.random.randint(key, (blocks, inner), 0, 65536) * ROWS_DEV + jnp.arange(inner, dtype=jnp.int32)[None, :]
    unused, chosen = lax.top_k(scores, SKETCH_DEV - 2)
    chosen = jnp.sort(chosen.astype(jnp.int32) + 1, axis=1)
    first = jnp.zeros((blocks, 1), jnp.int32)
    final = jnp.full((blocks, 1), ROWS_DEV - 1, jnp.int32)
    return jnp.concatenate([first, chosen, final], axis=1).reshape(-1).astype(jnp.int32)


def touch_ends(drawn, rng, low, high):
    longest = drawn.shape.index(max(drawn.shape))
    spots = []
    for shift in (0, 1):
        where = [jax.random.randint(jax.random.fold_in(rng, axis), (), 0, length) for axis, length in enumerate(drawn.shape)]
        where[longest] = (where[longest] + shift) % drawn.shape[longest]
        spots.append(tuple(where))
    return drawn.at[spots[0]].set(low).at[spots[1]].set(high)


def level_of(own_key, dims, shards, least, largest):
    loudness, own = 1.0, jax.random.fold_in(own_key, 6)
    for position, blocks in shards:
        steps = jnp.exp(jax.random.uniform(jax.random.fold_in(own, position), (blocks,), jnp.float32, least / len(shards), largest / len(shards)))
        loudness = loudness * jnp.repeat(steps, dims[position] // blocks).reshape([-1 if axis == position else 1 for axis in range(len(dims))])
    return loudness


def centred(key, extent, deviation, bound, split=(), kind=jnp.bfloat16):
    drawn = deviation * jax.random.normal(key, extent, jnp.float32)
    if split:
        drawn = drawn * level_of(key, extent, split, -0.22, 0.18)
    return jnp.clip(drawn, -bound, bound).astype(kind)


def setup_inputs(seed: int = 0) -> dict:
    key_list = jax.random.split(jax.random.key(seed), 6)
    return {
        "features": centred(key_list[0], (ROWS, D), 1.0, 6.0, ((0, 32), (1, 8))),
        "weights": centred(key_list[1], (D,), D ** -0.5, 0.0625, ((0, 8),), jnp.float32),
        "labels": touch_ends((jax.random.randint(key_list[2], (ROWS,), 0, 2) < 1).astype(jnp.int32), jax.random.fold_in(key_list[2], 1), 0, 1),
        "sign_bits": touch_ends((jax.random.randint(key_list[3], (ROWS,), 0, 2) < 1).astype(jnp.int32), jax.random.fold_in(key_list[3], 1), 0, 1),
        "sample_rows": draw_sample_rows(jax.random.fold_in(key_list[5], 71), 0),
    }


def sign_table(picked, size):
    levels = size.bit_length() - 1
    columns = jnp.arange(size, dtype=jnp.int32)
    parity = jnp.zeros((picked.shape[0], size), jnp.int32)
    for level in range(levels):
        left_bit = picked[:, None] // (1 << level) % 2
        right_bit = columns[None, :] // (1 << level) % 2
        parity = parity + left_bit * right_bit
    return (1 - 2 * (parity % 2)).astype(jnp.float32)

def reference(features, weights, labels, sign_bits, sample_rows):
    highest = lax.Precision.HIGHEST
    wide = features.astype(jnp.float32)
    logits = jnp.dot(wide, weights, precision=highest)
    probability = jax.nn.sigmoid(logits)
    residual = probability - labels.astype(jnp.float32)
    gradient = jnp.dot(residual, wide, precision=highest) / jnp.sqrt(jnp.float32(ROWS))
    scaling = (2 * sign_bits - 1).astype(jnp.float32) * jnp.sqrt(probability * (1.0 - probability))
    mixed_rows = (scaling[:, None] * wide).reshape(N_ROW, ROWS_DEV, D)
    block_table = sign_table(jnp.arange(N_ROW, dtype=jnp.int32), N_ROW)
    crossed = jnp.einsum('ab,bid->aid', block_table, mixed_rows, precision=highest)
    picked = sample_rows.reshape(N_ROW, SKETCH_DEV)

    def one_block(pair):
        rows_here, block = pair
        table = sign_table(rows_here, ROWS_DEV)
        return (jnp.dot(table, block, precision=highest) / jnp.sqrt(jnp.float32(ROWS))).astype(jnp.bfloat16)
    sketch = lax.map(one_block, (picked, crossed))

    def accumulate(total, block):
        partial_gram = lax.dot_general(block, block, (((0,), (0,)), ((), ())), preferred_element_type=jnp.float32)
        return (total + partial_gram, None)
    total, unused = lax.scan(accumulate, jnp.zeros((D, D), jnp.float32), sketch)
    gram = total / jnp.sqrt(jnp.float32(SKETCH))
    return (gram, gradient)
```

```python
import functools

import jax
import jax.numpy as jnp
from jax import lax
from jax.experimental import pallas as pl
from jax.experimental.pallas import tpu as pltpu
from jax.sharding import PartitionSpec as P

BF16, F32, I32 = jnp.bfloat16, jnp.float32, jnp.int32
MESH = pl.DeviceIdType.MESH

NX, NY, NZ, NZC = 4, 4, 8, 8
ROWS = 256
COLS = 896
OUT = 224
HALF = 448
DEPTH = ROWS * NZC
SKIP = 16
SKETCH = 7680
TOTAL = 8192


def nt(a, b):
    return lax.dot_general(a, b, (((1,), (1,)), ((), ())), preferred_element_type=F32)


def nn(a, b):
    return lax.dot_general(a, b, (((1,), (0,)), ((), ())), preferred_element_type=F32)


def split_rows(v):
    hi = v.astype(BF16).astype(F32)
    rest = v - hi
    mid = rest.astype(BF16).astype(F32)
    lo = rest - mid
    rid = lax.broadcasted_iota(I32, (8, v.shape[1]), 0)
    zero = jnp.zeros((8, v.shape[1]), F32)
    rows = jnp.where(rid == 0, hi, jnp.where(rid == 1, mid, jnp.where(rid == 2, lo, zero)))
    return rows.astype(BF16)


def kernel(
    x_ref, w_ref, lab_ref, sgn_ref, smp_ref, gram_ref, grad_ref,
    Z, Y, Ls, Lr, St, Ix, Cs, Cx, Cz, Czr, Cg, CT, Cy, Gb, Gown, Gr, Gs, Grr,
    zs, zr, cs, cr, ys, yr, ls, lr, ss, sr, ia_s, ia_r, ib_s, ib_r,
    cx_s, cx_r, cz_s, cz_r, cg_s, cg_r, cy_s, cy_r, g_s, g_r, d_s, d_r,
):
    row, feat = lax.axis_index("row"), lax.axis_index("feat")
    x, blk = row // NZC, row % NZC
    zh, c = blk // 2, blk % 2
    y, zl = feat // 2, feat % 2
    z = zh * 2 + zl
    q, h = zh // 2, zh % 2

    def dev(x_, z_, c_, y_):
        return (x_ * NZC + (z_ // 2) * 2 + c_, y_ * 2 + z_ % 2)

    def copy(src, dst, ssem, rsem, where):
        return pltpu.make_async_remote_copy(
            src_ref=src, dst_ref=dst, send_sem=ssem, recv_sem=rsem, device_id=where, device_id_type=MESH
        )

    here_other = dev(x, z, 1 - c, y)
    pending = []

    def send(src, dst, ssem, rsem, where):
        cp = copy(src, dst, ssem, rsem, where)
        cp.start()
        pending.append(cp)

    def arrived(dst, rsem):
        copy(dst, dst, rsem, rsem, here_other).wait_recv()

    def column(b):
        return pl.ds(pl.multiple_of(b * ROWS, ROWS), ROWS)

    def zc_dev(b):
        return dev(x, (b // 2) * 2 + zl, b % 2, y)

    Z[zl, :, column(blk)] = x_ref[...].T
    partial = jnp.sum(nt(split_rows(w_ref[...]), x_ref[...]), axis=0, keepdims=True)
    Ls[...] = jnp.broadcast_to(partial, (8, ROWS))
    order = lax.broadcasted_iota(I32, (SKIP, smp_ref.shape[1]), 1)
    rank = lax.broadcasted_iota(I32, (SKIP, smp_ref.shape[1]), 0)
    below = jnp.where(smp_ref[...] - order <= rank, 1.0, 0.0).astype(F32)
    skipped = jnp.sum(below, axis=1, keepdims=True)
    Ix[x, blk] = skipped + lax.broadcasted_iota(I32, (SKIP, 128), 0).astype(F32)

    barrier = pltpu.get_barrier_semaphore()
    greeted = []
    for dz in range(NZ):
        for other in range(2):
            if dz or other:
                greeted.append(dev(x, (z + dz) % NZ, (c + other) % 2, y))
    for dy in range(1, NY):
        greeted.append(dev(x, z, c, (y + dy) % NY))
        greeted.append(dev(x, z, 1 - c, (y + dy) % NY))
        greeted.append(dev(x, zh * 2 + 1 - zl, c, (y + dy) % NY))
    for dx in range(1, NX):
        greeted.append(dev((x + dx) % NX, z, c, y))
    for there in greeted:
        pl.semaphore_signal(barrier, inc=1, device_id=there, device_id_type=MESH)
    pl.semaphore_wait(barrier, len(greeted))

    for d in range(1, 8):
        other = (feat + d) % 8
        send(Ls, Lr.at[d - 1], ls.at[d - 1], lr.at[d - 1], (row, other))
    for d in range(1, NZC):
        b = (blk + d) % NZC
        send(Ix.at[x, blk], Ix.at[x, blk], ia_s.at[d - 1], ia_r.at[d - 1], zc_dev(b))

    def chunk(zsrc, core, j):
        b = (zsrc // 2) * 2 + core
        return Z.at[zsrc % 2, pl.ds(j * HALF, HALF), column(b)]

    def to_ring(i, step, j, zsrc):
        ref = chunk(zsrc, c, j)
        there = dev(x, (z + (1 - 2 * i)) % NZ, c, y)
        send(ref, ref, zs.at[i, step, j], zr.at[i, step, j], there)

    def y_copy(dy, core, zsrc_hi):
        b = zsrc_hi * 2 + c
        start = pl.multiple_of(h * HALF + core * OUT, 32)
        return copy(
            Z.at[q, pl.ds(start, OUT), column(b)],
            Y.at[dy - 1, :, column(b)],
            ys.at[dy - 1, core, zsrc_hi],
            yr.at[dy - 1, b],
            dev(x, z, core, (y + dy) % NY),
        )

    def to_y(zsrc, j):
        wanted = zsrc % 2 == q
        if j is not None:
            wanted = wanted & (h == j)

        @pl.when(wanted)
        def _():
            for dy in (1, 3, 2):
                for core in range(2):
                    y_copy(dy, core, zsrc // 2).start()

    for j in range(2):
        for i in range(2):
            to_ring(i, 0, j, z)
    own = Z.at[zl, :, column(blk)]
    send(own, own, cs.at[0, 4, 0], cr.at[0, 4, 0], here_other)
    to_y(z, None)

    logits = Ls[0:1, :]
    for d in range(1, 8):
        arrived(Lr.at[d - 1], lr.at[d - 1])
        logits = logits + Lr[d - 1, 0:1, :]
    prob = 1.0 / (1.0 + jnp.exp(-logits))
    var = prob * (1.0 - prob)
    resid = prob - lab_ref[...].astype(F32)
    scale = (2 * sgn_ref[...] - 1).astype(F32) * jnp.sqrt(var)
    rid8 = lax.broadcasted_iota(I32, (8, ROWS), 0)
    St[blk] = jnp.where(rid8 == 0, var, resid)
    for d in range(1, NZC):
        b = (blk + d) % NZC
        send(St.at[blk], St.at[blk], ss.at[d - 1], sr.at[d - 1], zc_dev(b))

    for d in range(1, NZC):
        b = (blk + NZC - d) % NZC
        arrived(Ix.at[x, b], ia_r.at[d - 1])
    for dx in range(1, NX):
        send(Ix.at[x], Ix.at[x], ib_s.at[dx - 1], ib_r.at[dx - 1], dev((x + dx) % NX, z, c, y))
    mixed = Z[zl, :, column(blk)].astype(F32) * scale
    mixed_hi = mixed.astype(BF16)
    mixed_lo = (mixed - mixed_hi.astype(F32)).astype(BF16)
    for dx in range(1, NX):
        arrived(Ix.at[(x + NX - dx) % NX], ib_r.at[dx - 1])

    def part_of_plane(plane, carry):
        index = Ix[plane].reshape(NZC * SKIP, 128).astype(I32)
        lane = lax.broadcasted_iota(I32, index.shape, 1)
        block = plane * NZC + lax.broadcasted_iota(I32, index.shape, 0) // SKIP
        low = (index & lane) | ((block & row) << 8)
        signs = []
        for u in (low, low | (index & 128)):
            u = u ^ (u >> 8)
            u = u ^ (u >> 4)
            u = u ^ (u >> 2)
            u = u ^ (u >> 1)
            signs.append((1 - 2 * (u & 1)).astype(F32))
        table = jnp.concatenate(signs, axis=1).astype(BF16)
        Cs[plane] = (nt(table, mixed_hi) + nt(table, mixed_lo)).astype(BF16)
        return carry

    lax.fori_loop(0, NX, part_of_plane, 0)
    for dx in range(1, NX):
        there = (x + dx) % NX
        send(Cs.at[there], Cx.at[dx - 1], cx_s.at[dx - 1], cx_r.at[dx - 1], dev(there, z, c, y))

    def ring_step(step, events):
        for i, j in events:
            zsrc = (z + NZ - (1 - 2 * i) * step) % NZ
            ref = chunk(zsrc, c, j)
            arrived(ref, zr.at[i, step - 1, j])
            if step < 3 or (step == 3 and i == j):
                to_ring(i, step, j, zsrc)
            send(ref, ref, cs.at[i, step - 1, j], cr.at[i, step - 1, j], here_other)
            to_y(zsrc, j)

    both = ((0, 0), (1, 0), (0, 1), (1, 1))
    ring_step(1, both)

    total = Cs[x].astype(F32)
    for dx in range(1, NX):
        arrived(Cx.at[dx - 1], cx_r.at[dx - 1])
        total = total + Cx[dx - 1].astype(F32)
    Cz[...] = total.astype(BF16)

    def sixteen(b):
        return pl.ds(pl.multiple_of(b * SKIP, SKIP), SKIP)

    for d in range(1, NZC):
        b = (blk + d) % NZC
        send(Cz.at[sixteen(b), :], Czr.at[d - 1], cz_s.at[d - 1], cz_r.at[d - 1], zc_dev(b))

    ring_step(2, both)

    total = Cz[sixteen(blk), :].astype(F32)
    for d in range(1, NZC):
        arrived(Czr.at[d - 1], cz_r.at[d - 1])
        total = total + Czr[d - 1].astype(F32)
    Cg[zl, sixteen(blk), :] = total.astype(BF16)
    mine = Cg.at[zl, sixteen(blk), :]
    for dz in range(NZ):
        for other in range(2):
            if dz or other:
                there = dev(x, (z + dz) % NZ, (c + other) % 2, y)
                send(mine, mine, cg_s.at[dz, other], cg_r.at[dz, other], there)

    ring_step(3, both)

    for dz in range(NZ):
        for other in range(2):
            if dz or other:
                zsrc = (z + NZ - dz) % NZ
                b = (zsrc // 2) * 2 + (c + other) % 2
                arrived(Cg.at[zsrc % 2, sixteen(b), :], cg_r.at[dz, other])
    CT[...] = Cg[q].T
    rows_here = pl.ds(pl.multiple_of(h * HALF + c * OUT, 32), OUT)
    for dy in range(1, NY):
        send(CT.at[rows_here, :], Cy.at[dy - 1], cy_s.at[dy - 1], cy_r.at[dy - 1], dev(x, z, c, (y + dy) % NY))

    ring_step(4, ((0, 0), (1, 1)))

    for d in range(1, NZC):
        arrived(St.at[(blk + NZC - d) % NZC], sr.at[d - 1])
    weight = jnp.concatenate([St[b, 0:1, :] for b in range(NZC)], axis=1)
    resids = jnp.concatenate([St[b, 1:2, :] for b in range(NZC)], axis=1)
    own_sib = Z.at[zl, :, column(zh * 2 + 1 - c)]
    arrived(own_sib, cr.at[0, 4, 0])
    for step in range(1, 5):
        for i, j in both if step < 4 else ((0, 0), (1, 1)):
            zsrc = (z + NZ - (1 - 2 * i) * step) % NZ
            arrived(chunk(zsrc, 1 - c, j), cr.at[i, step - 1, j])

    term = jnp.sum(nt(split_rows(resids), Z[zl]), axis=0, keepdims=True)
    Gs[...] = jnp.broadcast_to(term, (8, COLS))
    for dx in range(1, NX):
        send(Gs, Grr.at[dx - 1], d_s.at[dx - 1], d_r.at[dx - 1], dev((x + dx) % NX, z, c, y))

    for dy in (0, 1, 3, 2):
        if dy == 0:
            rows = Z[q, rows_here, :]
            skip = CT[rows_here, :]
        else:
            for b in range(NZC):
                arrived(Y.at[dy - 1, :, column(b)], yr.at[dy - 1, b])
            arrived(Cy.at[dy - 1], cy_r.at[dy - 1])
            rows = Y[dy - 1]
            skip = Cy[dy - 1]
        scaled = rows.astype(F32) * weight
        scaled_hi = scaled.astype(BF16)
        scaled_lo = (scaled - scaled_hi.astype(F32)).astype(BF16)
        block = nt(scaled_hi, Z[zl]) + nt(scaled_lo, Z[zl]) - nn(skip, Cg[zl]) * (1.0 / TOTAL)
        plane = (y + NY - dy) % NY

        @pl.when(plane == x)
        def _():
            Gown[...] = block

        @pl.when(plane != x)
        def _():
            Gb[dy] = block.astype(BF16)
            copy(Gb.at[dy], Gr.at[x], g_s.at[dy], g_r.at[x], dev(plane, z, c, y)).start()

    total = Gs[0:1, :]
    for dx in range(1, NX):
        arrived(Grr.at[dx - 1], d_r.at[dx - 1])
        total = total + Grr[dx - 1, 0:1, :]
    grad_ref[...] = total * (TOTAL ** -0.5)

    total = Gown[...]
    for dx in (1, 3, 2):
        src = (x + dx) % NX
        arrived(Gr.at[src], g_r.at[src])
        total = total + Gr[src].astype(F32)
    gram_ref[...] = total * (SKETCH ** -0.5)

    for cp in pending:
        cp.wait_send()
    for dy in range(1, NY):
        for core in range(2):
            for hi in range(4):
                y_copy(dy, core, hi).wait_send()
    for dy in range(NY):
        plane = (y + NY - dy) % NY

        @pl.when(plane != x)
        def _():
            copy(Gb.at[dy], Gr.at[x], g_s.at[dy], g_r.at[x], dev(plane, z, c, y)).wait_send()


def shards(features, weights, labels, sign_bits, sample_rows):
    vmem = pl.BlockSpec(memory_space=pltpu.VMEM)
    dma = pltpu.SemaphoreType.DMA
    scratch = [
        pltpu.VMEM((2, COLS, DEPTH), BF16),
        pltpu.VMEM((3, OUT, DEPTH), BF16),
        pltpu.VMEM((8, ROWS), F32),
        pltpu.VMEM((7, 8, ROWS), F32),
        pltpu.VMEM((NZC, 8, ROWS), F32),
        pltpu.VMEM((NX, NZC, SKIP, 128), F32),
        pltpu.VMEM((NX, NZC * SKIP, COLS), BF16),
        pltpu.VMEM((3, NZC * SKIP, COLS), BF16),
        pltpu.VMEM((NZC * SKIP, COLS), BF16),
        pltpu.VMEM((7, SKIP, COLS), BF16),
        pltpu.VMEM((2, NZC * SKIP, COLS), BF16),
        pltpu.VMEM((COLS, NZC * SKIP), BF16),
        pltpu.VMEM((3, OUT, NZC * SKIP), BF16),
        pltpu.VMEM((NY, OUT, COLS), BF16),
        pltpu.VMEM((OUT, COLS), F32),
        pltpu.VMEM((NX, OUT, COLS), BF16),
        pltpu.VMEM((8, COLS), F32),
        pltpu.VMEM((3, 8, COLS), F32),
        dma((2, 4, 2)), dma((2, 4, 2)),
        dma((2, 5, 2)), dma((2, 5, 2)),
        dma((3, 2, 4)), dma((3, 8)),
        dma((7,)), dma((7,)),
        dma((7,)), dma((7,)),
        dma((7,)), dma((7,)),
        dma((3,)), dma((3,)),
        dma((3,)), dma((3,)),
        dma((7,)), dma((7,)),
        dma((8, 2)), dma((8, 2)),
        dma((3,)), dma((3,)),
        dma((4,)), dma((4,)),
        dma((3,)), dma((3,)),
    ]
    gram, gradient = pl.pallas_call(
        kernel,
        out_shape=(
            jax.ShapeDtypeStruct((OUT, COLS), F32),
            jax.ShapeDtypeStruct((1, COLS), F32),
        ),
        in_specs=[vmem] * 5,
        out_specs=(vmem, vmem),
        scratch_shapes=scratch,
        compiler_params=pltpu.CompilerParams(
            collective_id=0, has_side_effects=True, vmem_limit_bytes=56 * 2**20
        ),
        name="newton_sketch",
    )(
        features,
        weights.reshape(1, -1),
        labels.reshape(1, -1),
        sign_bits.reshape(1, -1),
        sample_rows.reshape(1, -1),
    )
    return gram, gradient.reshape(-1)


def solution(mesh):
    placed = (P("row", "feat"), P("feat"), P("row"), P("row"), P("row"))
    return jax.shard_map(
        shards, mesh=mesh, in_specs=placed, out_specs=(P("row", "feat"), P("feat")), check_vma=False
    )
```

```python
import functools

import jax
import jax.numpy as jnp
from jax import lax
from jax.experimental import pallas as pl
from jax.experimental.pallas import tpu as pltpu
from jax.sharding import PartitionSpec as P

BF16, F32, I32 = jnp.bfloat16, jnp.float32, jnp.int32
MESH = pl.DeviceIdType.MESH

NX, NY, NZ, NZC = 4, 4, 8, 8
ROWS = 256
COLS = 896
OUT = 224
PART = (160, 64)
OFF = (0, 160)
BASE = (0, 640)
DEPTH = ROWS * NZC
SKIP = 16
SKETCH = 7680
TOTAL = 8192


def nt(a, b):
    return lax.dot_general(a, b, (((1,), (1,)), ((), ())), preferred_element_type=F32)


def nn(a, b):
    return lax.dot_general(a, b, (((1,), (0,)), ((), ())), preferred_element_type=F32)


def split_rows(v):
    hi = v.astype(BF16).astype(F32)
    rest = v - hi
    mid = rest.astype(BF16).astype(F32)
    lo = rest - mid
    rid = lax.broadcasted_iota(I32, (8, v.shape[1]), 0)
    zero = jnp.zeros((8, v.shape[1]), F32)
    rows = jnp.where(rid == 0, hi, jnp.where(rid == 1, mid, jnp.where(rid == 2, lo, zero)))
    return rows.astype(BF16)


def kernel(
    x_ref, w_ref, lab_ref, sgn_ref, smp_ref, gram_ref, grad_ref,
    Z, Y, Ls, Lr, St, Ix, Tb, Cs, Cx, Cg, CT, Cy, Gm, Gb, Gown, Gr, Gs, Grr,
    zs, zr, cs, cr, ys, yr, yf, ls, lr, ss, sr, ia_s, ia_r, ib_s, ib_r,
    cx_s, cx_r, cg_s, cg_r, cy_r, cp_s, g_s, g_r, d_s, d_r,
):
    row, feat = lax.axis_index("row"), lax.axis_index("feat")
    x, blk = row // NZC, row % NZC
    zh, c = blk // 2, blk % 2
    y, zl = feat // 2, feat % 2
    z = zh * 2 + zl
    q, h = zh // 2, zh % 2

    def dev(x_, z_, c_, y_):
        return (x_ * NZC + (z_ // 2) * 2 + c_, y_ * 2 + z_ % 2)

    here_other = dev(x, z, 1 - c, y)

    def zc_dev(b):
        return dev(x, (b // 2) * 2 + zl, b % 2, y)

    barrier = pltpu.get_barrier_semaphore()
    greeted = [zc_dev((blk + d) % NZC) for d in range(1, NZC)]
    greeted += [dev(x, (z + 1) % NZ, c, y), dev(x, (z + NZ - 1) % NZ, c, y)]
    for dy in range(1, NY):
        greeted.append(dev(x, z, c, (y + dy) % NY))
        greeted.append(dev(x, z, 1 - c, (y + dy) % NY))
        greeted.append(dev(x, zh * 2 + 1 - zl, c, (y + dy) % NY))
    for dx in range(1, NX):
        greeted.append(dev((x + dx) % NX, z, c, y))
    for there in greeted:
        pl.semaphore_signal(barrier, inc=1, device_id=there, device_id_type=MESH)

    def copy(src, dst, ssem, rsem, where):
        return pltpu.make_async_remote_copy(
            src_ref=src, dst_ref=dst, send_sem=ssem, recv_sem=rsem, device_id=where, device_id_type=MESH
        )

    pending = []

    def send(src, dst, ssem, rsem, where):
        cp = copy(src, dst, ssem, rsem, where)
        cp.start()
        pending.append(cp)

    def arrived(dst, rsem):
        copy(dst, dst, rsem, rsem, here_other).wait_recv()

    def column(b):
        return pl.ds(pl.multiple_of(b * ROWS, ROWS), ROWS)

    turned = x_ref[...].T
    for p in range(2):
        for g in range(4):
            Z[zl, pl.ds(BASE[p] + g * PART[p], PART[p]), column(blk)] = turned[
                g * OUT + OFF[p] : g * OUT + OFF[p] + PART[p]
            ]
    partial = jnp.sum(nt(split_rows(w_ref[...].reshape(1, COLS)), x_ref[...]), axis=0, keepdims=True)
    Ls[...] = jnp.broadcast_to(partial, (8, ROWS))
    order = lax.broadcasted_iota(I32, (SKIP, smp_ref.shape[0]), 1)
    rank = lax.broadcasted_iota(I32, (SKIP, smp_ref.shape[0]), 0)
    below = jnp.where(smp_ref[...].reshape(1, -1) - order <= rank, 1.0, 0.0).astype(F32)
    skipped = jnp.sum(below, axis=1, keepdims=True)
    Ix[x, blk] = skipped + lax.broadcasted_iota(I32, (SKIP, 128), 0).astype(F32)

    pl.semaphore_wait(barrier, len(greeted))

    for d in range(1, 8):
        send(Ls, Lr.at[d - 1], ls.at[d - 1], lr.at[d - 1], (row, (feat + d) % 8))
    for d in range(1, NZC):
        mine = Ix.at[x, blk]
        send(mine, mine, ia_s.at[d - 1], ia_r.at[d - 1], zc_dev((blk + d) % NZC))

    def chunk(zsrc, core, p, j):
        b = (zsrc // 2) * 2 + core
        return Z.at[zsrc % 2, pl.ds(BASE[p] + 2 * j * PART[p], 2 * PART[p]), column(b)]

    def to_ring(p, i, step, j, zsrc):
        ref = chunk(zsrc, c, p, j)
        there = dev(x, (z + (1 - 2 * i)) % NZ, c, y)
        send(ref, ref, zs.at[p, i, step, j], zr.at[p, i, step, j], there)

    def gram_rows(p, core):
        start = pl.multiple_of(BASE[p] + (2 * h + core) * PART[p], 32)
        return pl.ds(start, PART[p])

    def kept(p):
        return pl.ds(OFF[p], PART[p])

    def y_copy(p, way, core, zsrc_hi):
        dy = (1, 3)[way]
        b = zsrc_hi * 2 + c
        return copy(
            Z.at[q, gram_rows(p, core), column(b)],
            Y.at[dy - 1, kept(p), column(b)],
            ys.at[p, way, core, zsrc_hi],
            yr.at[p, dy - 1, b],
            dev(x, z, core, (y + dy) % NY),
        )

    def to_y(p, zsrc, j):
        wanted = zsrc % 2 == q
        if j is not None:
            wanted = wanted & (h == j)

        @pl.when(wanted)
        def _():
            for way in range(2):
                for core in range(2):
                    y_copy(p, way, core, zsrc // 2).start()

    sg = 1 - 2 * h
    pieces = [
        (jnp.where(q == zl, z + a, z + b) + NZ) % NZ
        for a, b in ((0, -sg), (-2 * sg, sg), (2 * sg, -3 * sg), (4, 3 * sg))
    ]

    def y_forward(p, k):
        for way in range(2):
            b = (pieces[k] // 2) * 2 + way
            slot = 2 * way
            ref = Y.at[slot, kept(p), column(b)]
            arrived(ref, yr.at[p, slot, b])
            there = dev(x, z, c, (y + (1, 3)[way]) % NY)
            send(ref, Y.at[1, kept(p), column(b)], yf.at[p, way, k], yr.at[p, 1, b], there)

    def ring_start(p):
        for jj in range(2):
            for i in range(2):
                to_ring(p, i, 0, jj if i == 0 else 1 - jj, z)
        own = Z.at[zl, pl.ds(BASE[p], 4 * PART[p]), column(blk)]
        send(own, own, cs.at[p, 0, 4, 0], cr.at[p, 0, 4, 0], here_other)
        to_y(p, z, None)

    def ring_event(p, step, jj):
        for i in range(2):
            j = jj if i == 0 else 1 - jj
            zsrc = (z + NZ - (1 - 2 * i) * step) % NZ
            ref = chunk(zsrc, c, p, j)
            arrived(ref, zr.at[p, i, step - 1, j])
            if step < 3 or (step == 3 and jj == 0):
                to_ring(p, i, step, j, zsrc)
            send(ref, ref, cs.at[p, i, step - 1, j], cr.at[p, i, step - 1, j], here_other)
            to_y(p, zsrc, j)

    def sibling_arrived(p):
        own = Z.at[zl, pl.ds(BASE[p], 4 * PART[p]), column(zh * 2 + 1 - c)]
        arrived(own, cr.at[p, 0, 4, 0])
        for step in range(1, 5):
            for jj in range(2 if step < 4 else 1):
                for i in range(2):
                    j = jj if i == 0 else 1 - jj
                    zsrc = (z + NZ - (1 - 2 * i) * step) % NZ
                    arrived(chunk(zsrc, 1 - c, p, j), cr.at[p, i, step - 1, j])

    ring_start(0)

    logits = Ls[0:1, :]
    for d in range(1, 8):
        arrived(Lr.at[d - 1], lr.at[d - 1])
        logits = logits + Lr[d - 1, 0:1, :]
    prob = 1.0 / (1.0 + jnp.exp(-logits))
    var = prob * (1.0 - prob)
    resid = prob - lab_ref[...].reshape(1, ROWS).astype(F32)
    scale = (2 * sgn_ref[...].reshape(1, ROWS) - 1).astype(F32) * jnp.sqrt(var)
    rid8 = lax.broadcasted_iota(I32, (8, ROWS), 0)
    St[blk] = jnp.where(rid8 == 0, var, jnp.where(rid8 == 1, resid, scale))
    for d in range(1, NZC):
        send(St.at[blk], St.at[blk], ss.at[d - 1], sr.at[d - 1], zc_dev((blk + d) % NZC))

    ring_event(0, 1, 0)

    for d in range(1, NZC):
        arrived(Ix.at[x, (blk + NZC - d) % NZC], ia_r.at[d - 1])
    for dx in range(1, NX):
        send(Ix.at[x], Ix.at[x], ib_s.at[dx - 1], ib_r.at[dx - 1], dev((x + dx) % NX, z, c, y))

    ring_event(0, 1, 1)
    ring_event(0, 2, 0)
    y_forward(0, 0)

    for dx in range(1, NX):
        arrived(Ix.at[(x + NX - dx) % NX], ib_r.at[dx - 1])
    index = jnp.concatenate([Ix[u, 2 * v + c] for u in range(NX) for v in range(4)], axis=0).astype(I32)
    lane = lax.broadcasted_iota(I32, index.shape, 1)
    place = lax.broadcasted_iota(I32, index.shape, 0) // SKIP
    block = (place // 4) * NZC + (place % 4) * 2 + c

    def parity(u):
        u = u ^ (u >> 8)
        u = u ^ (u >> 4)
        u = u ^ (u >> 2)
        u = u ^ (u >> 1)
        return u & 1

    low = parity(index & lane)
    high = low ^ ((index >> 7) & 1)
    for b in range(NZC):
        flip = parity(block & (x * NZC + b))
        for part, bits in enumerate((low, high)):
            Tb[:, b * ROWS + part * 128 : b * ROWS + part * 128 + 128] = (1 - 2 * (bits ^ flip)).astype(F32).astype(BF16)

    ring_event(0, 2, 1)
    ring_event(0, 3, 0)
    y_forward(0, 1)
    ring_event(0, 3, 1)
    ring_start(1)

    for d in range(1, NZC):
        arrived(St.at[(blk + NZC - d) % NZC], sr.at[d - 1])
    weight = jnp.concatenate([St[b, 0:1, :] for b in range(NZC)], axis=1)
    resids = jnp.concatenate([St[b, 1:2, :] for b in range(NZC)], axis=1)
    scales = jnp.concatenate([St[b, 2:3, :] for b in range(NZC)], axis=1)

    def out_copy(dy, p, shape):
        plane = (y + NY - dy) % NY
        if shape == 0:
            where = (pl.ds(0, OFF[p]), pl.ds(BASE[p], 4 * PART[p]))
        else:
            where = (kept(p), pl.ds(0, BASE[p] + 4 * PART[p]))
        return copy(
            Gb.at[(dy,) + where], Gr.at[(x,) + where],
            g_s.at[dy, p, shape], g_r.at[x, p, shape], dev(plane, z, c, y),
        )

    def pieces_of(p, shape):
        if shape == 0:
            return tuple(range(p)), pl.ds(BASE[p], 4 * PART[p])
        return (p,), pl.ds(0, BASE[p] + 4 * PART[p])

    def product(dy, p, shape):
        parts, cols = pieces_of(p, shape)
        for r in parts:
            rows = Z[q, gram_rows(r, c), :] if dy == 0 else Y[dy - 1, kept(r), :]
            scaled = rows.astype(F32) * weight
            scaled_hi = scaled.astype(BF16)
            scaled_lo = (scaled - scaled_hi.astype(F32)).astype(BF16)
            both = nt(jnp.concatenate([scaled_hi, scaled_lo], axis=0), Z[zl, cols, :])
            Gm[dy, kept(r), cols] = both[: PART[r]] + both[PART[r] :]

    def finish(dy, p, shape):
        parts, cols = pieces_of(p, shape)
        plane = (y + NY - dy) % NY
        for r in parts:
            block = Gm[dy, kept(r), cols] - nn(Cy[dy, kept(r), :], Cg[:, cols]) * (1.0 / TOTAL)

            @pl.when(plane == x)
            def _():
                Gown[kept(r), cols] = block

            @pl.when(plane != x)
            def _():
                Gb[dy, kept(r), cols] = block.astype(BF16)

        @pl.when(plane != x)
        def _():
            out_copy(dy, p, shape).start()

    def y_arrived(p, dy):
        for b in range(NZC):
            if dy == 2 or b % 2 == (1 if dy == 1 else 0):
                arrived(Y.at[dy - 1, kept(p), column(b)], yr.at[p, dy - 1, b])

    def features(p):
        return pl.ds(BASE[p], 4 * PART[p])

    def half_rows(core):
        return pl.ds(pl.multiple_of(core * 4 * SKIP, 4 * SKIP), 4 * SKIP)

    def plane_rows(u):
        return pl.ds(pl.multiple_of(u * 4 * SKIP, 4 * SKIP), 4 * SKIP)

    def skipped_part(p):
        mixed = (Z[zl, features(p), :].astype(F32) * scales).astype(BF16)
        Cs[:, features(p)] = nt(Tb[...], mixed).astype(BF16)
        for dx in (2, 1, 3):
            there = (x + dx) % NX
            send(
                Cs.at[plane_rows(there), features(p)], Cx.at[dx - 1, :, features(p)],
                cx_s.at[p, dx - 1], cx_r.at[p, dx - 1], dev(there, z, c, y),
            )

    def skipped_sum(p):
        total = Cs[plane_rows(x), features(p)].astype(F32)
        for dx in range(1, NX):
            arrived(Cx.at[dx - 1, :, features(p)], cx_r.at[p, dx - 1])
            total = total + Cx[dx - 1, :, features(p)].astype(F32)
        mine = Cg.at[half_rows(c), features(p)]
        mine[...] = total.astype(BF16)
        send(mine, mine, cg_s.at[p], cg_r.at[p], here_other)

    def c_copy(p, dy, far):
        there = dev(x, zh * 2 + (1 - zl if far else zl), c, (y + dy) % NY)
        return copy(
            CT.at[gram_rows(p, c), :], Cy.at[dy, kept(p), :], cp_s.at[p, dy, far], cy_r.at[p, dy], there
        )

    c_targets = [(dy, far) for dy in (1, 3, 2, 0) for far in range(2) if dy or far]

    def skipped_spread(p):
        arrived(Cg.at[half_rows(1 - c), features(p)], cg_r.at[p])

        @pl.when(q == zl)
        def _():
            CT[features(p), :] = Cg[:, features(p)].T
            for dy, far in c_targets:
                c_copy(p, dy, far).start()
            Cy[0, kept(p), :] = CT[gram_rows(p, c), :]

    def skipped_arrived(p, dy):
        if dy:
            arrived(Cy.at[dy, kept(p), :], cy_r.at[p, dy])
        else:

            @pl.when(q != zl)
            def _():
                arrived(Cy.at[dy, kept(p), :], cy_r.at[p, dy])

    ring_event(0, 4, 0)
    y_forward(0, 2)
    sibling_arrived(0)
    skipped_part(0)
    ring_event(1, 1, 0)
    ring_event(1, 1, 1)
    product(0, 0, 1)
    ring_event(1, 2, 0)
    y_forward(0, 3)
    ring_event(1, 2, 1)
    skipped_sum(0)
    ring_event(1, 3, 0)
    y_forward(1, 0)
    y_arrived(0, 1)
    product(1, 0, 1)
    ring_event(1, 3, 1)
    skipped_spread(0)
    y_forward(1, 1)
    y_arrived(0, 3)
    product(3, 0, 1)
    ring_event(1, 4, 0)
    sibling_arrived(1)
    skipped_part(1)
    y_forward(1, 2)
    skipped_arrived(0, 0)
    finish(0, 0, 1)
    y_forward(1, 3)
    y_arrived(0, 2)
    product(2, 0, 1)
    for dy in (1, 3, 2):
        skipped_arrived(0, dy)
        finish(dy, 0, 1)
    skipped_sum(1)
    term = jnp.sum(nt(split_rows(resids), Z[zl]), axis=0, keepdims=True)
    Gs[...] = jnp.broadcast_to(term, (8, COLS))
    for dx in range(1, NX):
        send(Gs, Grr.at[dx - 1], d_s.at[dx - 1], d_r.at[dx - 1], dev((x + dx) % NX, z, c, y))
    product(0, 1, 0)
    skipped_spread(1)
    finish(0, 1, 0)
    for dy in (1, 3, 2):
        product(dy, 1, 0)
        finish(dy, 1, 0)
    product(0, 1, 1)
    skipped_arrived(1, 0)
    finish(0, 1, 1)
    for dy in (1, 3, 2):
        y_arrived(1, dy)
        product(dy, 1, 1)
        skipped_arrived(1, dy)
        finish(dy, 1, 1)

    def natural(v):
        cuts = []
        for g in range(4):
            for p in range(2):
                start = BASE[p] + g * PART[p]
                cuts.append(v[:, start : start + PART[p]])
        return jnp.concatenate(cuts, axis=1)

    total = Gs[...]
    for dx in range(1, NX):
        arrived(Grr.at[dx - 1], d_r.at[dx - 1])
        total = total + Grr[dx - 1]
    grad_ref[...] = (natural(total)[0:1, :] * (TOTAL ** -0.5)).reshape(COLS)

    for dx in (1, 3, 2):
        src = (x + dx) % NX
        for p, shape in ((0, 1), (1, 0), (1, 1)):
            if shape == 0:
                where = (pl.ds(0, OFF[p]), pl.ds(BASE[p], 4 * PART[p]))
            else:
                where = (kept(p), pl.ds(0, BASE[p] + 4 * PART[p]))
            arrived(Gr.at[(src,) + where], g_r.at[src, p, shape])
    total = Gown[...]
    for dx in range(1, NX):
        total = total + Gr[(x + dx) % NX].astype(F32)
    gram_ref[...] = natural(total) * (SKETCH ** -0.5)

    for cp in pending:
        cp.wait_send()
    for p in range(2):
        for way in range(2):
            for core in range(2):
                for hi in range(4):
                    y_copy(p, way, core, hi).wait_send()
    @pl.when(q == zl)
    def _():
        for p in range(2):
            for dy, far in c_targets:
                c_copy(p, dy, far).wait_send()

    for dy in range(NY):

        @pl.when((y + NY - dy) % NY != x)
        def _():
            for p, shape in ((0, 1), (1, 0), (1, 1)):
                out_copy(dy, p, shape).wait_send()


def shards(features, weights, labels, sign_bits, sample_rows):
    vmem = pl.BlockSpec(memory_space=pltpu.VMEM)
    dma = pltpu.SemaphoreType.DMA
    scratch = [
        pltpu.VMEM((2, COLS, DEPTH), BF16),
        pltpu.VMEM((3, OUT, DEPTH), BF16),
        pltpu.VMEM((8, ROWS), F32),
        pltpu.VMEM((7, 8, ROWS), F32),
        pltpu.VMEM((NZC, 8, ROWS), F32),
        pltpu.VMEM((NX, NZC, SKIP, 128), F32),
        pltpu.VMEM((NX * 4 * SKIP, DEPTH), BF16),
        pltpu.VMEM((NX * 4 * SKIP, COLS), BF16),
        pltpu.VMEM((3, 4 * SKIP, COLS), BF16),
        pltpu.VMEM((NZC * SKIP, COLS), BF16),
        pltpu.VMEM((COLS, NZC * SKIP), BF16),
        pltpu.VMEM((NY, OUT, NZC * SKIP), BF16),
        pltpu.VMEM((NY, OUT, COLS), F32),
        pltpu.VMEM((NY, OUT, COLS), BF16),
        pltpu.VMEM((OUT, COLS), F32),
        pltpu.VMEM((NX, OUT, COLS), BF16),
        pltpu.VMEM((8, COLS), F32),
        pltpu.VMEM((3, 8, COLS), F32),
        dma((2, 2, 4, 2)), dma((2, 2, 4, 2)),
        dma((2, 2, 5, 2)), dma((2, 2, 5, 2)),
        dma((2, 2, 2, 4)), dma((2, 3, 8)), dma((2, 2, 4)),
        dma((7,)), dma((7,)),
        dma((7,)), dma((7,)),
        dma((7,)), dma((7,)),
        dma((3,)), dma((3,)),
        dma((2, 3)), dma((2, 3)),
        dma((2,)), dma((2,)),
        dma((2, 4)), dma((2, 4, 2)),
        dma((4, 2, 2)), dma((4, 2, 2)),
        dma((3,)), dma((3,)),
    ]
    gram, gradient = pl.pallas_call(
        kernel,
        out_shape=(
            jax.ShapeDtypeStruct((OUT, COLS), F32),
            jax.ShapeDtypeStruct((COLS,), F32),
        ),
        in_specs=[vmem] * 5,
        out_specs=(vmem, vmem),
        scratch_shapes=scratch,
        compiler_params=pltpu.CompilerParams(
            collective_id=0, has_side_effects=True, vmem_limit_bytes=56 * 2**20
        ),
        name="newton_sketch",
    )(
        features, weights, labels, sign_bits, sample_rows
    )
    return gram, gradient


def solution(mesh):
    placed = (P("row", "feat"), P("feat"), P("row"), P("row"), P("row"))
    return jax.shard_map(
        shards, mesh=mesh, in_specs=placed, out_specs=(P("row", "feat"), P("feat")), check_vma=False
    )
```

```python
import functools

import jax
import jax.numpy as jnp
from jax import lax
from jax.experimental import pallas as pl
from jax.experimental.pallas import tpu as pltpu
from jax.sharding import PartitionSpec as P

BF16, F32, I32 = jnp.bfloat16, jnp.float32, jnp.int32
MESH = pl.DeviceIdType.MESH

NX, NY, NZ, NZC = 4, 4, 8, 8
ROWS = 256
COLS = 896
OUT = 224
PART = (128, 96)
OFF = (0, 128)
BASE = (0, 512)
DEPTH = ROWS * NZC
SKIP = 16
SKETCH = 7680
TOTAL = 8192
TABLE = 256
HEAD = TABLE + 16


def nt(a, b):
    return lax.dot_general(a, b, (((1,), (1,)), ((), ())), preferred_element_type=F32)


def nn(a, b):
    return lax.dot_general(a, b, (((1,), (0,)), ((), ())), preferred_element_type=F32)


def split_rows(v):
    hi = v.astype(BF16).astype(F32)
    rest = v - hi
    mid = rest.astype(BF16).astype(F32)
    lo = rest - mid
    rid = lax.broadcasted_iota(I32, (16, v.shape[1]), 0)
    zero = jnp.zeros((16, v.shape[1]), F32)
    rows = jnp.where(rid == 0, hi, jnp.where(rid == 1, mid, jnp.where(rid == 2, lo, zero)))
    return rows.astype(BF16)


def kernel(
    x_ref, w_ref, lab_ref, sgn_ref, smp_ref, gram_ref, grad_ref,
    Z, Y, Ls, Lr, St, Ix, La, Lb, Cs, Cx, Cg, CT, Cy, Gm, Gb, Gown, Gr, Gs, Grr,
    zs, zr, cs, cr, ys, yr, y2, yf, ls, lr, ss, sr, ia_s, ia_r, ib_s, ib_r,
    cx_s, cx_r, cg_s, cg_r, cy_r, cy_s, g_s, g_r, d_s, d_r,
):
    row, feat = lax.axis_index("row"), lax.axis_index("feat")
    x, blk = row // NZC, row % NZC
    zh, c = blk // 2, blk % 2
    y, zl = feat // 2, feat % 2
    z = zh * 2 + zl
    q, h = zh // 2, zh % 2

    def dev(x_, z_, c_, y_):
        return (x_ * NZC + (z_ // 2) * 2 + c_, y_ * 2 + z_ % 2)

    here_other = dev(x, z, 1 - c, y)

    def zc_dev(b):
        return dev(x, (b // 2) * 2 + zl, b % 2, y)

    barrier = pltpu.get_barrier_semaphore()
    greeted = [zc_dev((blk + d) % NZC) for d in range(1, NZC)]
    greeted += [dev(x, (z + 1) % NZ, c, y), dev(x, (z + NZ - 1) % NZ, c, y)]
    for dy in range(1, NY):
        greeted.append(dev(x, z, c, (y + dy) % NY))
        greeted.append(dev(x, z, 1 - c, (y + dy) % NY))
        greeted.append(dev(x, zh * 2 + 1 - zl, c, (y + dy) % NY))
    for dx in range(1, NX):
        greeted.append(dev((x + dx) % NX, z, c, y))
    for there in greeted:
        pl.semaphore_signal(barrier, inc=1, device_id=there, device_id_type=MESH)

    def copy(src, dst, ssem, rsem, where):
        return pltpu.make_async_remote_copy(
            src_ref=src, dst_ref=dst, send_sem=ssem, recv_sem=rsem, device_id=where, device_id_type=MESH
        )

    def send(src, dst, ssem, rsem, where):
        copy(src, dst, ssem, rsem, where).start()

    def arrived(dst, rsem):
        copy(dst, dst, rsem, rsem, here_other).wait_recv()

    def departed(src, ssem):
        copy(src, src, ssem, ssem, here_other).wait_send()

    def column(b):
        return pl.ds(pl.multiple_of(b * ROWS, ROWS), ROWS)

    turned = x_ref[...].T
    for p in range(2):
        for g in range(4):
            Z[zl, pl.ds(BASE[p] + g * PART[p], PART[p]), column(blk)] = turned[
                g * OUT + OFF[p] : g * OUT + OFF[p] + PART[p]
            ]
    partial = jnp.sum(nt(split_rows(w_ref[...].reshape(1, COLS)), x_ref[...]), axis=0, keepdims=True)
    Ls[...] = jnp.broadcast_to(partial, (8, ROWS))
    order = lax.broadcasted_iota(I32, (SKIP, smp_ref.shape[0]), 1)
    rank = lax.broadcasted_iota(I32, (SKIP, smp_ref.shape[0]), 0)
    below = jnp.where(smp_ref[...].reshape(1, -1) - order <= rank, 1.0, 0.0).astype(F32)
    skipped = jnp.sum(below, axis=1, keepdims=True)
    Ix[x, blk] = skipped + lax.broadcasted_iota(I32, (SKIP, 128), 0).astype(F32)

    pl.semaphore_wait(barrier, len(greeted))

    for d in range(1, 8):
        send(Ls, Lr.at[d - 1], ls.at[0], lr.at[0], (row, (feat + d) % 8))
    for d in range(1, NZC):
        mine = Ix.at[x, blk]
        send(mine, mine, ia_s.at[0], ia_r.at[0], zc_dev((blk + d) % NZC))

    def chunk(zsrc, core, p, j):
        b = (zsrc // 2) * 2 + core
        return Z.at[zsrc % 2, pl.ds(BASE[p] + 2 * j * PART[p], 2 * PART[p]), column(b)]

    def to_ring(p, i, step, j, zsrc):
        ref = chunk(zsrc, c, p, j)
        there = dev(x, (z + (1 - 2 * i)) % NZ, c, y)
        send(ref, ref, zs.at[p], zr.at[p, i, step, j], there)

    def gram_rows(p, core):
        start = pl.multiple_of(BASE[p] + (2 * h + core) * PART[p], 32)
        return pl.ds(start, PART[p])

    def kept(p):
        return pl.ds(OFF[p], PART[p])

    def y_copy(p, way, core, zsrc_hi):
        dy = (1, 3)[way]
        b = zsrc_hi * 2 + c
        return copy(
            Z.at[q, gram_rows(p, core), column(b)],
            Y.at[dy - 1, kept(p), column(b)],
            ys.at[p],
            yr.at[p, way, jnp.where(c == way, zsrc_hi, 4)],
            dev(x, z, core, (y + dy) % NY),
        )

    def to_y(p, zsrc, j):
        wanted = zsrc % 2 == q
        if j is not None:
            wanted = wanted & (h == j)

        @pl.when(wanted)
        def _():
            for way in range(2):
                for core in range(2):
                    y_copy(p, way, core, zsrc // 2).start()

    sg = 1 - 2 * h
    pieces = [
        (jnp.where(q == zl, z + a, z + b) + NZ) % NZ
        for a, b in ((0, -sg), (-2 * sg, sg), (2 * sg, -3 * sg), (4, 3 * sg))
    ]

    def y_forward(p, k):
        for way in range(2):
            b = (pieces[k] // 2) * 2 + way
            slot = 2 * way
            ref = Y.at[slot, kept(p), column(b)]
            arrived(ref, yr.at[p, way, pieces[k] // 2])
            there = dev(x, z, c, (y + (1, 3)[way]) % NY)
            send(ref, Y.at[1, kept(p), column(b)], yf.at[p], y2.at[p], there)

    def ring_start(p):
        for jj in range(2):
            for i in range(2):
                to_ring(p, i, 0, jj if i == 0 else 1 - jj, z)
        own = Z.at[zl, pl.ds(BASE[p], 4 * PART[p]), column(blk)]
        send(own, own, cs.at[p], cr.at[p], here_other)
        to_y(p, z, None)

    def ring_event(p, step, jj):
        for i in range(2):
            j = jj if i == 0 else 1 - jj
            zsrc = (z + NZ - (1 - 2 * i) * step) % NZ
            ref = chunk(zsrc, c, p, j)
            arrived(ref, zr.at[p, i, step - 1, j])
            if step < 3 or (step == 3 and jj == 0):
                to_ring(p, i, step, j, zsrc)
            send(ref, ref, cs.at[p], cr.at[p], here_other)
            to_y(p, zsrc, j)

    def sibling_arrived(p):
        arrived(Z.at[zl, pl.ds(BASE[p], 4 * PART[p]), :], cr.at[p])

    ring_start(0)

    logits = Ls[0:1, :]
    arrived(Lr, lr.at[0])
    for d in range(1, 8):
        logits = logits + Lr[d - 1, 0:1, :]
    prob = 1.0 / (1.0 + jnp.exp(-logits))
    var = prob * (1.0 - prob)
    resid = prob - lab_ref[...].reshape(1, ROWS).astype(F32)
    scale = (2 * sgn_ref[...].reshape(1, ROWS) - 1).astype(F32) * jnp.sqrt(var)
    rid8 = lax.broadcasted_iota(I32, (8, ROWS), 0)
    St[blk] = jnp.where(rid8 == 0, var, jnp.where(rid8 == 1, resid, scale))
    for d in range(1, NZC):
        send(St.at[blk], St.at[blk], ss.at[0], sr.at[0], zc_dev((blk + d) % NZC))

    ring_event(0, 1, 0)

    arrived(Ix.at[x, 0:7], ia_r.at[0])
    for dx in range(1, NX):
        send(Ix.at[x], Ix.at[x], ib_s.at[0], ib_r.at[0], dev((x + dx) % NX, z, c, y))

    ring_event(0, 1, 1)
    ring_event(0, 2, 0)
    y_forward(0, 0)

    arrived(Ix.at[0:3], ib_r.at[0])
    index = jnp.concatenate([Ix[u, 2 * v + c] for u in range(NX) for v in range(4)], axis=0).astype(I32)
    lane = lax.broadcasted_iota(I32, index.shape, 1)
    place = lax.broadcasted_iota(I32, index.shape, 0) // SKIP
    block = (place // 4) * NZC + (place % 4) * 2 + c

    def parity(u):
        u = u ^ (u >> 8)
        u = u ^ (u >> 4)
        u = u ^ (u >> 2)
        u = u ^ (u >> 1)
        return u & 1

    low = parity(index & lane)
    high = low ^ ((index >> 7) & 1)
    for b in range(NZC):
        flip = parity(block & (x * NZC + b))
        for part, bits in enumerate((low, high)):
            La[0:TABLE, b * ROWS + part * 128 : b * ROWS + part * 128 + 128] = (1 - 2 * (bits ^ flip)).astype(F32).astype(BF16)

    ring_event(0, 2, 1)
    ring_event(0, 3, 0)
    y_forward(0, 1)
    ring_event(0, 3, 1)
    ring_start(1)

    arrived(St.at[0:7], sr.at[0])
    weight = jnp.concatenate([St[b, 0:1, :] for b in range(NZC)], axis=1)
    resids = jnp.concatenate([St[b, 1:2, :] for b in range(NZC)], axis=1)
    scales = jnp.concatenate([St[b, 2:3, :] for b in range(NZC)], axis=1)

    def out_copy(dy, p, shape):
        plane = (y + NY - dy) % NY
        if shape == 0:
            where = (pl.ds(0, OFF[p]), pl.ds(BASE[p], 4 * PART[p]))
        else:
            where = (kept(p), pl.ds(0, BASE[p] + 4 * PART[p]))
        return copy(
            Gb.at[(dy,) + where], Gr.at[(x,) + where],
            g_s.at[p, shape], g_r.at[p, shape], dev(plane, z, c, y),
        )

    def pieces_of(p, shape):
        if shape == 0:
            return tuple(range(p)), pl.ds(BASE[p], 4 * PART[p])
        return (p,), pl.ds(0, BASE[p] + 4 * PART[p])

    def features(p):
        return pl.ds(BASE[p], 4 * PART[p])

    def left(dy, start, height):
        if dy == 0:
            return La.at[HEAD + start : HEAD + start + height]
        return Lb.at[dy - 1, start : start + height]

    def prepare(dy, p):
        rows = Z[q, gram_rows(p, c), :] if dy == 0 else Y[dy - 1, kept(p), :]
        scaled = rows.astype(F32) * weight
        high = scaled.astype(BF16)
        left(dy, 2 * OFF[p], PART[p])[...] = high
        left(dy, 2 * OFF[p] + PART[p], PART[p])[...] = (scaled - high.astype(F32)).astype(BF16)

    def product(dy, p):
        both = nt(left(dy, 0, 2 * PART[0])[...], Z[zl, features(p), :])
        Gm[dy, kept(0), features(p)] = both[: PART[0]] + both[PART[0] :]

    def product_last(dy):
        for p in range(2):
            both = nt(left(dy, 2 * OFF[1], 2 * PART[1])[...], Z[zl, features(p), :])
            Gm[dy, kept(1), features(p)] = both[: PART[1]] + both[PART[1] :]

    def product_own(p):
        all_rows = nt(La[0 : HEAD + 2 * PART[0]], Z[zl, features(p), :])
        Cs[:, features(p)] = all_rows[:TABLE].astype(BF16)
        for dx in (2, 1, 3):
            there = (x + dx) % NX
            send(
                Cs.at[plane_rows(there), features(p)], Cx.at[dx - 1, :, features(p)],
                cx_s.at[p], cx_r.at[p], dev(there, z, c, y),
            )
        Gs[:, features(p)] = jnp.broadcast_to(
            jnp.sum(all_rows[TABLE:HEAD], axis=0, keepdims=True), (8, 4 * PART[p])
        )
        Gm[0, kept(0), features(p)] = all_rows[HEAD : HEAD + PART[0]] + all_rows[HEAD + PART[0] :]

    def finish(dy, p, shape):
        parts, cols = pieces_of(p, shape)
        plane = (y + NY - dy) % NY
        for r in parts:
            block = Gm[dy, kept(r), cols] - nn(Cy[dy, kept(r), :], Cg[:, cols]) * (1.0 / TOTAL)

            @pl.when(plane == x)
            def _():
                Gown[kept(r), cols] = block

            @pl.when(plane != x)
            def _():
                Gb[dy, kept(r), cols] = block.astype(BF16)

        @pl.when(plane != x)
        def _():
            out_copy(dy, p, shape).start()

    def y_arrived(p, dy):
        if dy == 2:
            arrived(Y.at[1, kept(p), :], y2.at[p])
        else:
            arrived(Y.at[dy - 1, kept(p), 0 : DEPTH // 2], yr.at[p, dy // 2, 4])

    def half_rows(core):
        return pl.ds(pl.multiple_of(core * 4 * SKIP, 4 * SKIP), 4 * SKIP)

    def plane_rows(u):
        return pl.ds(pl.multiple_of(u * 4 * SKIP, 4 * SKIP), 4 * SKIP)

    def skipped_sum(p):
        total = Cs[plane_rows(x), features(p)].astype(F32)
        arrived(Cx.at[:, :, features(p)], cx_r.at[p])
        for dx in range(1, NX):
            total = total + Cx[dx - 1, :, features(p)].astype(F32)
        mine = Cg.at[half_rows(c), features(p)]
        mine[...] = total.astype(BF16)
        send(mine, mine, cg_s.at[p], cg_r.at[p], here_other)

    def c_copy(p, dy, far):
        there = dev(x, zh * 2 + (1 - zl if far else zl), c, (y + dy) % NY)
        return copy(
            CT.at[gram_rows(p, c), :], Cy.at[dy, kept(p), :], cy_s.at[p, far], cy_r.at[p, dy], there
        )

    c_targets = [(dy, far) for dy in (1, 3, 2, 0) for far in range(2) if dy or far]

    def skipped_spread(p):
        arrived(Cg.at[half_rows(1 - c), features(p)], cg_r.at[p])

        @pl.when(q == zl)
        def _():
            CT[features(p), :] = Cg[:, features(p)].T
            for dy, far in c_targets:
                c_copy(p, dy, far).start()
            Cy[0, kept(p), :] = CT[gram_rows(p, c), :]

    def skipped_arrived(p, dy):
        if dy:
            arrived(Cy.at[dy, kept(p), :], cy_r.at[p, dy])
        else:

            @pl.when(q != zl)
            def _():
                arrived(Cy.at[dy, kept(p), :], cy_r.at[p, dy])

    La[0:TABLE] = (La[0:TABLE].astype(F32) * scales).astype(BF16)
    La[TABLE:HEAD] = split_rows(resids)
    ring_event(0, 4, 0)
    y_forward(0, 2)
    sibling_arrived(0)
    prepare(0, 0)
    product_own(0)
    ring_event(1, 1, 0)
    ring_event(1, 1, 1)
    ring_event(1, 2, 0)
    y_forward(0, 3)
    ring_event(1, 2, 1)
    skipped_sum(0)
    ring_event(1, 3, 0)
    y_forward(1, 0)
    y_arrived(0, 1)
    prepare(1, 0)
    product(1, 0)
    ring_event(1, 3, 1)
    skipped_spread(0)
    y_arrived(0, 3)
    prepare(3, 0)
    product(3, 0)
    ring_event(1, 4, 0)
    y_forward(1, 1)
    sibling_arrived(1)
    product_own(1)
    for dx in range(1, NX):
        send(Gs, Grr.at[dx - 1], d_s.at[0], d_r.at[0], dev((x + dx) % NX, z, c, y))
    skipped_arrived(0, 0)
    finish(0, 0, 1)
    for dy in (1, 3):
        skipped_arrived(0, dy)
        finish(dy, 0, 1)
    y_forward(1, 2)
    y_forward(1, 3)
    y_arrived(0, 2)
    prepare(2, 0)
    product(2, 0)
    skipped_arrived(0, 2)
    finish(2, 0, 1)
    skipped_sum(1)
    product(1, 1)
    product(3, 1)
    product(2, 1)
    skipped_spread(1)
    for dy in (0, 1, 3, 2):
        finish(dy, 1, 0)
    prepare(0, 1)
    product_last(0)
    skipped_arrived(1, 0)
    finish(0, 1, 1)
    for dy in (1, 3, 2):
        y_arrived(1, dy)
        prepare(dy, 1)
        product_last(dy)
        skipped_arrived(1, dy)
        finish(dy, 1, 1)

    def natural(v):
        cuts = []
        for g in range(4):
            for p in range(2):
                start = BASE[p] + g * PART[p]
                cuts.append(v[:, start : start + PART[p]])
        return jnp.concatenate(cuts, axis=1)

    departed(Lr, ls.at[0])
    departed(Ix.at[x, 0:7], ia_s.at[0])
    departed(Ix.at[0:3], ib_s.at[0])
    departed(St.at[0:7], ss.at[0])
    for p in range(2):
        departed(Z.at[0, features(p), 0 : 7 * ROWS], zs.at[p])
        departed(Z.at[0, features(p), :], cs.at[p])
        departed(Y.at[0:2, kept(p), :], ys.at[p])
        departed(Y.at[0, kept(p), :], yf.at[p])
        departed(Cx.at[:, :, features(p)], cx_s.at[p])
        departed(Cg.at[half_rows(c), features(p)], cg_s.at[p])

    @pl.when(q == zl)
    def _():
        for p in range(2):
            departed(Cy.at[0:3, kept(p), :], cy_s.at[p, 0])
            departed(Cy.at[:, kept(p), :], cy_s.at[p, 1])

    total = Gs[...]
    arrived(Grr, d_r.at[0])
    for dx in range(1, NX):
        total = total + Grr[dx - 1]
    grad_ref[...] = (natural(total)[0:1, :] * (TOTAL ** -0.5)).reshape(COLS)
    departed(Grr, d_s.at[0])

    regions = []
    for p, shape in ((0, 1), (1, 0), (1, 1)):
        if shape == 0:
            where = (pl.ds(0, OFF[p]), pl.ds(BASE[p], 4 * PART[p]))
        else:
            where = (kept(p), pl.ds(0, BASE[p] + 4 * PART[p]))
        regions.append((p, shape, (pl.ds(0, 3),) + where))
    for p, shape, where in regions:
        arrived(Gr.at[where], g_r.at[p, shape])
    total = Gown[...]
    for dx in range(1, NX):
        total = total + Gr[(x + dx) % NX].astype(F32)
    gram_ref[...] = natural(total) * (SKETCH ** -0.5)
    for p, shape, where in regions:
        departed(Gb.at[where], g_s.at[p, shape])


def shards(features, weights, labels, sign_bits, sample_rows):
    vmem = pl.BlockSpec(memory_space=pltpu.VMEM)
    dma = pltpu.SemaphoreType.DMA
    scratch = [
        pltpu.VMEM((2, COLS, DEPTH), BF16),
        pltpu.VMEM((3, OUT, DEPTH), BF16),
        pltpu.VMEM((8, ROWS), F32),
        pltpu.VMEM((7, 8, ROWS), F32),
        pltpu.VMEM((NZC, 8, ROWS), F32),
        pltpu.VMEM((NX, NZC, SKIP, 128), F32),
        pltpu.VMEM((HEAD + 2 * OUT, DEPTH), BF16),
        pltpu.VMEM((3, 2 * OUT, DEPTH), BF16),
        pltpu.VMEM((NX * 4 * SKIP, COLS), BF16),
        pltpu.VMEM((3, 4 * SKIP, COLS), BF16),
        pltpu.VMEM((NZC * SKIP, COLS), BF16),
        pltpu.VMEM((COLS, NZC * SKIP), BF16),
        pltpu.VMEM((NY, OUT, NZC * SKIP), BF16),
        pltpu.VMEM((NY, OUT, COLS), F32),
        pltpu.VMEM((NY, OUT, COLS), BF16),
        pltpu.VMEM((OUT, COLS), F32),
        pltpu.VMEM((NX, OUT, COLS), BF16),
        pltpu.VMEM((8, COLS), F32),
        pltpu.VMEM((3, 8, COLS), F32),
        dma((2,)), dma((2, 2, 4, 2)),
        dma((2,)), dma((2,)),
        dma((2,)), dma((2, 2, 5)), dma((2,)), dma((2,)),
        dma((1,)), dma((1,)),
        dma((1,)), dma((1,)),
        dma((1,)), dma((1,)),
        dma((1,)), dma((1,)),
        dma((2,)), dma((2,)),
        dma((2,)), dma((2,)),
        dma((2, 4)), dma((2, 2)),
        dma((2, 2)), dma((2, 2)),
        dma((1,)), dma((1,)),
    ]
    gram, gradient = pl.pallas_call(
        kernel,
        out_shape=(
            jax.ShapeDtypeStruct((OUT, COLS), F32),
            jax.ShapeDtypeStruct((COLS,), F32),
        ),
        in_specs=[vmem] * 5,
        out_specs=(vmem, vmem),
        scratch_shapes=scratch,
        compiler_params=pltpu.CompilerParams(
            collective_id=0, has_side_effects=True, vmem_limit_bytes=56 * 2**20
        ),
        name="newton_sketch",
    )(
        features, weights, labels, sign_bits, sample_rows
    )
    return gram, gradient


def solution(mesh):
    placed = (P("row", "feat"), P("feat"), P("row"), P("row"), P("row"))
    return jax.shard_map(
        shards, mesh=mesh, in_specs=placed, out_specs=(P("row", "feat"), P("feat")), check_vma=False
    )
```

```python
import functools

import jax
import jax.numpy as jnp
from jax import lax
from jax.experimental import pallas as pl
from jax.experimental.pallas import tpu as pltpu
from jax.sharding import PartitionSpec as P

BF16, F32, I32 = jnp.bfloat16, jnp.float32, jnp.int32
MESH = pl.DeviceIdType.MESH

NX, NY, NZ, NZC = 4, 4, 8, 8
ROWS = 256
COLS = 896
OUT = 224
PART = (128, 96)
OFF = (0, 128)
BASE = (0, 512)
DEPTH = ROWS * NZC
SKIP = 16
SKETCH = 7680
TOTAL = 8192
TABLE = 256
HEAD = TABLE + 16


def nt(a, b):
    return lax.dot_general(a, b, (((1,), (1,)), ((), ())), preferred_element_type=F32)


def nn(a, b):
    return lax.dot_general(a, b, (((1,), (0,)), ((), ())), preferred_element_type=F32)


def split_rows(v):
    hi = v.astype(BF16).astype(F32)
    rest = v - hi
    mid = rest.astype(BF16).astype(F32)
    lo = rest - mid
    rid = lax.broadcasted_iota(I32, (16, v.shape[1]), 0)
    zero = jnp.zeros((16, v.shape[1]), F32)
    rows = jnp.where(rid == 0, hi, jnp.where(rid == 1, mid, jnp.where(rid == 2, lo, zero)))
    return rows.astype(BF16)


def kernel(
    x_ref, w_ref, lab_ref, sgn_ref, smp_ref, gram_ref, grad_ref,
    Z, Y, Ls, Lr, St, Ix, La, Lb, Cs, Cx, Cg, CT, Cy, Gm, Gb, Gown, Gf, Gr, Gs, Grr,
    zs, zr, cs, cr, ys, yr, y2, yf, ls, lr, ss, sr, ia_s, ia_r, ib_s, ib_r,
    cx_s, cx_r, cg_s, cg_r, cy_r, cy_s, g_s, g_r, f_s, f_r, d_s, d_r,
):
    row, feat = lax.axis_index("row"), lax.axis_index("feat")
    x, blk = row // NZC, row % NZC
    zh, c = blk // 2, blk % 2
    y, zl = feat // 2, feat % 2
    z = zh * 2 + zl
    q, h = zh // 2, zh % 2

    def dev(x_, z_, c_, y_):
        return (x_ * NZC + (z_ // 2) * 2 + c_, y_ * 2 + z_ % 2)

    here_other = dev(x, z, 1 - c, y)

    def zc_dev(b):
        return dev(x, (b // 2) * 2 + zl, b % 2, y)

    barrier = pltpu.get_barrier_semaphore()
    greeted = [zc_dev((blk + d) % NZC) for d in range(1, NZC)]
    greeted += [dev(x, (z + 1) % NZ, c, y), dev(x, (z + NZ - 1) % NZ, c, y)]
    for dy in range(1, NY):
        greeted.append(dev(x, z, c, (y + dy) % NY))
        greeted.append(dev(x, z, 1 - c, (y + dy) % NY))
        greeted.append(dev(x, zh * 2 + 1 - zl, c, (y + dy) % NY))
    for dx in range(1, NX):
        greeted.append(dev((x + dx) % NX, z, c, y))
    for there in greeted:
        pl.semaphore_signal(barrier, inc=1, device_id=there, device_id_type=MESH)

    def copy(src, dst, ssem, rsem, where):
        return pltpu.make_async_remote_copy(
            src_ref=src, dst_ref=dst, send_sem=ssem, recv_sem=rsem, device_id=where, device_id_type=MESH
        )

    def send(src, dst, ssem, rsem, where):
        copy(src, dst, ssem, rsem, where).start()

    def arrived(dst, rsem):
        copy(dst, dst, rsem, rsem, here_other).wait_recv()

    def departed(src, ssem):
        copy(src, src, ssem, ssem, here_other).wait_send()

    def column(b):
        return pl.ds(pl.multiple_of(b * ROWS, ROWS), ROWS)

    turned = x_ref[...].T
    for p in range(2):
        for g in range(4):
            Z[zl, pl.ds(BASE[p] + g * PART[p], PART[p]), column(blk)] = turned[
                g * OUT + OFF[p] : g * OUT + OFF[p] + PART[p]
            ]
    partial = jnp.sum(nt(split_rows(w_ref[...].reshape(1, COLS)), x_ref[...]), axis=0, keepdims=True)
    Ls[...] = jnp.broadcast_to(partial, (8, ROWS))
    order = lax.broadcasted_iota(I32, (SKIP, smp_ref.shape[0]), 1)
    rank = lax.broadcasted_iota(I32, (SKIP, smp_ref.shape[0]), 0)
    below = jnp.where(smp_ref[...].reshape(1, -1) - order <= rank, 1.0, 0.0).astype(F32)
    skipped = jnp.sum(below, axis=1, keepdims=True)
    Ix[x, blk] = skipped + lax.broadcasted_iota(I32, (SKIP, 128), 0).astype(F32)

    pl.semaphore_wait(barrier, len(greeted))

    for d in range(1, 8):
        send(Ls, Lr.at[d - 1], ls.at[0], lr.at[0], (row, (feat + d) % 8))
    for d in range(1, NZC):
        mine = Ix.at[x, blk]
        send(mine, mine, ia_s.at[0], ia_r.at[0], zc_dev((blk + d) % NZC))

    def chunk(zsrc, core, p, j):
        b = (zsrc // 2) * 2 + core
        return Z.at[zsrc % 2, pl.ds(BASE[p] + 2 * j * PART[p], 2 * PART[p]), column(b)]

    def to_ring(p, i, step, j, zsrc):
        ref = chunk(zsrc, c, p, j)
        there = dev(x, (z + (1 - 2 * i)) % NZ, c, y)
        send(ref, ref, zs.at[p], zr.at[p, i, step, j], there)

    def gram_rows(p, core):
        start = pl.multiple_of(BASE[p] + (2 * h + core) * PART[p], 32)
        return pl.ds(start, PART[p])

    def kept(p):
        return pl.ds(OFF[p], PART[p])

    def y_copy(p, way, core, zsrc_hi):
        dy = (1, 3)[way]
        b = zsrc_hi * 2 + c
        return copy(
            Z.at[q, gram_rows(p, core), column(b)],
            Y.at[dy - 1, kept(p), column(b)],
            ys.at[p],
            yr.at[p, way, jnp.where(c == way, zsrc_hi, 4)],
            dev(x, z, core, (y + dy) % NY),
        )

    def to_y(p, zsrc, j):
        wanted = zsrc % 2 == q
        if j is not None:
            wanted = wanted & (h == j)

        @pl.when(wanted)
        def _():
            for way in range(2):
                for core in range(2):
                    y_copy(p, way, core, zsrc // 2).start()

    sg = 1 - 2 * h
    pieces = [
        (jnp.where(q == zl, z + a, z + b) + NZ) % NZ
        for a, b in ((0, -sg), (-2 * sg, sg), (2 * sg, -3 * sg), (4, 3 * sg))
    ]

    def y_forward(p, k):
        for way in range(2):
            b = (pieces[k] // 2) * 2 + way
            slot = 2 * way
            ref = Y.at[slot, kept(p), column(b)]
            arrived(ref, yr.at[p, way, pieces[k] // 2])
            there = dev(x, z, c, (y + (1, 3)[way]) % NY)
            send(ref, Y.at[1, kept(p), column(b)], yf.at[p], y2.at[p], there)

    def ring_start(p):
        for jj in range(2):
            for i in range(2):
                to_ring(p, i, 0, jj if i == 0 else 1 - jj, z)
        own = Z.at[zl, pl.ds(BASE[p], 4 * PART[p]), column(blk)]
        send(own, own, cs.at[p], cr.at[p], here_other)
        to_y(p, z, None)

    def ring_event(p, step, jj):
        for i in range(2):
            j = jj if i == 0 else 1 - jj
            zsrc = (z + NZ - (1 - 2 * i) * step) % NZ
            ref = chunk(zsrc, c, p, j)
            arrived(ref, zr.at[p, i, step - 1, j])
            if step < 3 or (step == 3 and jj == 0):
                to_ring(p, i, step, j, zsrc)
            send(ref, ref, cs.at[p], cr.at[p], here_other)
            to_y(p, zsrc, j)

    def sibling_arrived(p):
        arrived(Z.at[zl, pl.ds(BASE[p], 4 * PART[p]), :], cr.at[p])

    ring_start(0)

    ring_event(0, 1, 0)
    ring_event(0, 1, 1)

    logits = Ls[0:1, :]
    arrived(Lr, lr.at[0])
    for d in range(1, 8):
        logits = logits + Lr[d - 1, 0:1, :]
    prob = 1.0 / (1.0 + jnp.exp(-logits))
    var = prob * (1.0 - prob)
    resid = prob - lab_ref[...].reshape(1, ROWS).astype(F32)
    scale = (2 * sgn_ref[...].reshape(1, ROWS) - 1).astype(F32) * jnp.sqrt(var)
    rid8 = lax.broadcasted_iota(I32, (8, ROWS), 0)
    St[blk] = jnp.where(rid8 == 0, var, jnp.where(rid8 == 1, resid, scale))
    for d in range(1, NZC):
        send(St.at[blk], St.at[blk], ss.at[0], sr.at[0], zc_dev((blk + d) % NZC))

    arrived(Ix.at[x, 0:7], ia_r.at[0])
    for dx in range(1, NX):
        send(Ix.at[x], Ix.at[x], ib_s.at[0], ib_r.at[0], dev((x + dx) % NX, z, c, y))

    ring_event(0, 2, 0)
    y_forward(0, 0)

    arrived(Ix.at[0:3], ib_r.at[0])
    index = jnp.concatenate([Ix[u, 2 * v + c] for u in range(NX) for v in range(4)], axis=0).astype(I32)
    lane = lax.broadcasted_iota(I32, index.shape, 1)
    place = lax.broadcasted_iota(I32, index.shape, 0) // SKIP
    block = (place // 4) * NZC + (place % 4) * 2 + c

    def parity(u):
        u = u ^ (u >> 8)
        u = u ^ (u >> 4)
        u = u ^ (u >> 2)
        u = u ^ (u >> 1)
        return u & 1

    low = parity(index & lane)
    high = low ^ ((index >> 7) & 1)
    for b in range(NZC):
        flip = parity(block & (x * NZC + b))
        for part, bits in enumerate((low, high)):
            La[0:TABLE, b * ROWS + part * 128 : b * ROWS + part * 128 + 128] = (1 - 2 * (bits ^ flip)).astype(F32).astype(BF16)

    ring_event(0, 2, 1)
    ring_event(0, 3, 0)
    y_forward(0, 1)
    ring_event(0, 3, 1)
    ring_start(1)

    arrived(St.at[0:7], sr.at[0])
    weight = jnp.concatenate([St[b, 0:1, :] for b in range(NZC)], axis=1)
    resids = jnp.concatenate([St[b, 1:2, :] for b in range(NZC)], axis=1)
    scales = jnp.concatenate([St[b, 2:3, :] for b in range(NZC)], axis=1)

    def region(p, shape, half=None):
        start, height = (0, OFF[p]) if shape == 0 else (OFF[p], PART[p])
        width = (BASE[p], 4 * PART[p]) if shape == 0 else (0, BASE[p] + 4 * PART[p])
        if half is not None:
            start, height = start + half * (height // 2), height // 2
        return (pl.ds(start, height), pl.ds(*width))

    def features(p):
        return pl.ds(BASE[p], 4 * PART[p])

    def left(dy, start, height):
        if dy == 0:
            return La.at[HEAD + start : HEAD + start + height]
        return Lb.at[dy - 1, start : start + height]

    def prepare(dy, p):
        rows = Z[q, gram_rows(p, c), :] if dy == 0 else Y[dy - 1, kept(p), :]
        scaled = rows.astype(F32) * weight
        high = scaled.astype(BF16)
        left(dy, 2 * OFF[p], PART[p])[...] = high
        left(dy, 2 * OFF[p] + PART[p], PART[p])[...] = (scaled - high.astype(F32)).astype(BF16)

    def product(dy, p):
        both = nt(left(dy, 0, 2 * PART[0])[...], Z[zl, features(p), :])
        Gm[dy, kept(0), features(p)] = both[: PART[0]] + both[PART[0] :]

    def product_rest():
        height = 2 * PART[0]
        rows = jnp.concatenate([left(dy, 0, height)[...] for dy in range(1, NY)], axis=0)
        all_rows = nt(rows, Z[zl, features(1), :])
        for dy in range(1, NY):
            one = all_rows[(dy - 1) * height : dy * height]
            Gm[dy, kept(0), features(1)] = one[: PART[0]] + one[PART[0] :]

    def product_last():
        height = 2 * PART[1]
        rows = jnp.concatenate([left(dy, 2 * OFF[1], height)[...] for dy in range(NY)], axis=0)
        for p in range(2):
            all_rows = nt(rows, Z[zl, features(p), :])
            for dy in range(NY):
                one = all_rows[dy * height : (dy + 1) * height]
                Gm[dy, kept(1), features(p)] = one[: PART[1]] + one[PART[1] :]

    def product_own(p):
        all_rows = nt(La[0 : HEAD + 2 * PART[0]], Z[zl, features(p), :])
        Cs[:, features(p)] = all_rows[:TABLE].astype(BF16)
        for dx in (2, 1, 3):
            there = (x + dx) % NX
            send(
                Cs.at[plane_rows(there), features(p)], Cx.at[dx - 1, :, features(p)],
                cx_s.at[p], cx_r.at[p], dev(there, z, c, y),
            )
        Gs[:, features(p)] = jnp.broadcast_to(
            jnp.sum(all_rows[TABLE:HEAD], axis=0, keepdims=True), (8, 4 * PART[p])
        )
        Gm[0, kept(0), features(p)] = all_rows[HEAD : HEAD + PART[0]] + all_rows[HEAD + PART[0] :]

    def corrected(dx, where):
        dy = (y - x - dx + 2 * NY) % NY
        return Gm[(dy,) + where] - nn(Cy[dy, where[0], :], Cg[:, where[1]]) * (1.0 / TOTAL)

    def finish_far(p, shape):
        whole = region(p, shape)
        Gb[(1,) + whole] = corrected(2, whole).astype(BF16)
        for half in range(2):
            where = region(p, shape, half)
            there = dev((x + 1 + 2 * half) % NX, z, c, y)
            send(Gb.at[(1,) + where], Gf.at[where], f_s.at[p, shape], f_r.at[p, shape], there)
        Gown[whole] = corrected(0, whole)

    def finish_near(p, shape):
        whole = region(p, shape)
        arrived(Gf.at[whole], f_r.at[p, shape])
        for half in range(2):
            dx = 1 + 2 * half
            added, plain = region(p, shape, half), region(p, shape, 1 - half)
            Gb[(2 * half,) + added] = (corrected(dx, added) + Gf[added].astype(F32)).astype(BF16)
            Gb[(2 * half,) + plain] = corrected(dx, plain).astype(BF16)
            send(
                Gb.at[(2 * half,) + whole], Gr.at[(half,) + whole],
                g_s.at[p, shape], g_r.at[p, shape], dev((x + dx) % NX, z, c, y),
            )

    def y_arrived(p, dy):
        if dy == 2:
            arrived(Y.at[1, kept(p), :], y2.at[p])
        else:
            arrived(Y.at[dy - 1, kept(p), 0 : DEPTH // 2], yr.at[p, dy // 2, 4])

    def half_rows(core):
        return pl.ds(pl.multiple_of(core * 4 * SKIP, 4 * SKIP), 4 * SKIP)

    def plane_rows(u):
        return pl.ds(pl.multiple_of(u * 4 * SKIP, 4 * SKIP), 4 * SKIP)

    def skipped_sum(p):
        total = Cs[plane_rows(x), features(p)].astype(F32)
        arrived(Cx.at[:, :, features(p)], cx_r.at[p])
        for dx in range(1, NX):
            total = total + Cx[dx - 1, :, features(p)].astype(F32)
        mine = Cg.at[half_rows(c), features(p)]
        mine[...] = total.astype(BF16)
        send(mine, mine, cg_s.at[p], cg_r.at[p], here_other)

    def c_copy(p, dy, far):
        there = dev(x, zh * 2 + (1 - zl if far else zl), c, (y + dy) % NY)
        return copy(
            CT.at[gram_rows(p, c), :], Cy.at[dy, kept(p), :], cy_s.at[p, far], cy_r.at[p, dy], there
        )

    c_targets = [(dy, far) for dy in (1, 3, 2, 0) for far in range(2) if dy or far]

    def skipped_spread(p):
        arrived(Cg.at[half_rows(1 - c), features(p)], cg_r.at[p])

        @pl.when(q == zl)
        def _():
            CT[features(p), :] = Cg[:, features(p)].T
            for dy, far in c_targets:
                c_copy(p, dy, far).start()
            Cy[0, kept(p), :] = CT[gram_rows(p, c), :]

    def skipped_arrived(p, dy):
        if dy:
            arrived(Cy.at[dy, kept(p), :], cy_r.at[p, dy])
        else:

            @pl.when(q != zl)
            def _():
                arrived(Cy.at[dy, kept(p), :], cy_r.at[p, dy])

    La[0:TABLE] = (La[0:TABLE].astype(F32) * scales).astype(BF16)
    La[TABLE:HEAD] = split_rows(resids)
    ring_event(0, 4, 0)
    y_forward(0, 2)
    sibling_arrived(0)
    prepare(0, 0)
    product_own(0)
    ring_event(1, 1, 0)
    ring_event(1, 1, 1)
    ring_event(1, 2, 0)
    y_forward(0, 3)
    ring_event(1, 2, 1)
    skipped_sum(0)
    ring_event(1, 3, 0)
    y_forward(1, 0)
    y_arrived(0, 1)
    prepare(1, 0)
    product(1, 0)
    ring_event(1, 3, 1)
    skipped_spread(0)
    y_arrived(0, 3)
    prepare(3, 0)
    product(3, 0)
    ring_event(1, 4, 0)
    y_forward(1, 1)
    sibling_arrived(1)
    product_own(1)
    for dx in range(1, NX):
        send(Gs, Grr.at[dx - 1], d_s.at[0], d_r.at[0], dev((x + dx) % NX, z, c, y))
    y_arrived(0, 2)
    prepare(2, 0)
    product(2, 0)
    for dy in range(NY):
        skipped_arrived(0, dy)
    finish_far(0, 1)
    y_forward(1, 2)
    y_forward(1, 3)
    product_rest()
    skipped_sum(1)
    prepare(0, 1)
    y_arrived(1, 1)
    prepare(1, 1)
    skipped_spread(1)
    finish_near(0, 1)
    finish_far(1, 0)
    for dy in (3, 2):
        y_arrived(1, dy)
        prepare(dy, 1)
    product_last()
    for dy in range(NY):
        skipped_arrived(1, dy)
    finish_far(1, 1)
    finish_near(1, 0)

    def natural(v):
        cuts = []
        for g in range(4):
            for p in range(2):
                start = BASE[p] + g * PART[p]
                cuts.append(v[:, start : start + PART[p]])
        return jnp.concatenate(cuts, axis=1)

    departed(Lr, ls.at[0])
    departed(Ix.at[x, 0:7], ia_s.at[0])
    departed(Ix.at[0:3], ib_s.at[0])
    departed(St.at[0:7], ss.at[0])
    for p in range(2):
        departed(Z.at[0, features(p), 0 : 7 * ROWS], zs.at[p])
        departed(Z.at[0, features(p), :], cs.at[p])
        departed(Y.at[0:2, kept(p), :], ys.at[p])
        departed(Y.at[0, kept(p), :], yf.at[p])
        departed(Cx.at[:, :, features(p)], cx_s.at[p])
        departed(Cg.at[half_rows(c), features(p)], cg_s.at[p])

    @pl.when(q == zl)
    def _():
        for p in range(2):
            departed(Cy.at[0:3, kept(p), :], cy_s.at[p, 0])
            departed(Cy.at[:, kept(p), :], cy_s.at[p, 1])

    total = Gs[...]
    arrived(Grr, d_r.at[0])
    for dx in range(1, NX):
        total = total + Grr[dx - 1]
    grad_ref[...] = (natural(total)[0:1, :] * (TOTAL ** -0.5)).reshape(COLS)
    departed(Grr, d_s.at[0])

    finish_near(1, 1)
    regions = [(0, 1), (1, 0), (1, 1)]
    for p, shape in regions:
        arrived(Gr.at[(slice(None),) + region(p, shape)], g_r.at[p, shape])
    total = Gown[...] + Gr[0].astype(F32) + Gr[1].astype(F32)
    gram_ref[...] = natural(total) * (SKETCH ** -0.5)
    for p, shape in regions:
        departed(Gb.at[(1,) + region(p, shape)], f_s.at[p, shape])
        departed(Gr.at[(slice(None),) + region(p, shape)], g_s.at[p, shape])


def shards(features, weights, labels, sign_bits, sample_rows):
    vmem = pl.BlockSpec(memory_space=pltpu.VMEM)
    dma = pltpu.SemaphoreType.DMA
    scratch = [
        pltpu.VMEM((2, COLS, DEPTH), BF16),
        pltpu.VMEM((3, OUT, DEPTH), BF16),
        pltpu.VMEM((8, ROWS), F32),
        pltpu.VMEM((7, 8, ROWS), F32),
        pltpu.VMEM((NZC, 8, ROWS), F32),
        pltpu.VMEM((NX, NZC, SKIP, 128), F32),
        pltpu.VMEM((HEAD + 2 * OUT, DEPTH), BF16),
        pltpu.VMEM((3, 2 * OUT, DEPTH), BF16),
        pltpu.VMEM((NX * 4 * SKIP, COLS), BF16),
        pltpu.VMEM((3, 4 * SKIP, COLS), BF16),
        pltpu.VMEM((NZC * SKIP, COLS), BF16),
        pltpu.VMEM((COLS, NZC * SKIP), BF16),
        pltpu.VMEM((NY, OUT, NZC * SKIP), BF16),
        pltpu.VMEM((NY, OUT, COLS), F32),
        pltpu.VMEM((3, OUT, COLS), BF16),
        pltpu.VMEM((OUT, COLS), F32),
        pltpu.VMEM((OUT, COLS), BF16),
        pltpu.VMEM((2, OUT, COLS), BF16),
        pltpu.VMEM((8, COLS), F32),
        pltpu.VMEM((3, 8, COLS), F32),
        dma((2,)), dma((2, 2, 4, 2)),
        dma((2,)), dma((2,)),
        dma((2,)), dma((2, 2, 5)), dma((2,)), dma((2,)),
        dma((1,)), dma((1,)),
        dma((1,)), dma((1,)),
        dma((1,)), dma((1,)),
        dma((1,)), dma((1,)),
        dma((2,)), dma((2,)),
        dma((2,)), dma((2,)),
        dma((2, 4)), dma((2, 2)),
        dma((2, 2)), dma((2, 2)),
        dma((2, 2)), dma((2, 2)),
        dma((1,)), dma((1,)),
    ]
    gram, gradient = pl.pallas_call(
        kernel,
        out_shape=(
            jax.ShapeDtypeStruct((OUT, COLS), F32),
            jax.ShapeDtypeStruct((COLS,), F32),
        ),
        in_specs=[vmem] * 5,
        out_specs=(vmem, vmem),
        scratch_shapes=scratch,
        compiler_params=pltpu.CompilerParams(
            collective_id=0, has_side_effects=True, vmem_limit_bytes=56 * 2**20
        ),
        name="newton_sketch",
    )(
        features, weights, labels, sign_bits, sample_rows
    )
    return gram, gradient


def solution(mesh):
    placed = (P("row", "feat"), P("feat"), P("row"), P("row"), P("row"))
    return jax.shard_map(
        shards, mesh=mesh, in_specs=placed, out_specs=(P("row", "feat"), P("feat")), check_vma=False
    )
```

```python
import functools

import jax
import jax.numpy as jnp
from jax import lax
from jax.experimental import pallas as pl
from jax.experimental.pallas import tpu as pltpu
from jax.sharding import PartitionSpec as P

BF16, F32, I32 = jnp.bfloat16, jnp.float32, jnp.int32
MESH = pl.DeviceIdType.MESH

NX, NY, NZ, NZC = 4, 4, 8, 8
ROWS = 256
COLS = 896
OUT = 224
PART = (128, 96)
OFF = (0, 128)
BASE = (0, 512)
DEPTH = ROWS * NZC
SKIP = 16
SKETCH = 7680
TOTAL = 8192
TABLE = 256
HEAD = TABLE + 16


def nt(a, b):
    return lax.dot_general(a, b, (((1,), (1,)), ((), ())), preferred_element_type=F32)


def nn(a, b):
    return lax.dot_general(a, b, (((1,), (0,)), ((), ())), preferred_element_type=F32)


def split_rows(v):
    hi = v.astype(BF16).astype(F32)
    rest = v - hi
    mid = rest.astype(BF16).astype(F32)
    lo = rest - mid
    rid = lax.broadcasted_iota(I32, (16, v.shape[1]), 0)
    zero = jnp.zeros((16, v.shape[1]), F32)
    rows = jnp.where(rid == 0, hi, jnp.where(rid == 1, mid, jnp.where(rid == 2, lo, zero)))
    return rows.astype(BF16)


def kernel(
    x_ref, w_ref, lab_ref, sgn_ref, smp_ref, gram_ref, grad_ref,
    Z, Y, Ls, Lr, St, Ix, La, Lb, Cs, Cx, Cg, CT, Cy, Gm, Gb, Gown, Gf, Gr, Gs, Grr,
    zs, zr, cs, cr, ys, yr, y2, yf, ls, lr, ss, sr, ia_s, ia_r, ib_s, ib_r,
    cx_s, cx_r, cg_s, cg_r, cy_r, cy_s, g_s, g_r, f_s, f_r, d_s, d_r,
):
    row, feat = lax.axis_index("row"), lax.axis_index("feat")
    x, blk = row // NZC, row % NZC
    zh, c = blk // 2, blk % 2
    y, zl = feat // 2, feat % 2
    z = zh * 2 + zl
    q, h = zh // 2, zh % 2

    def dev(x_, z_, c_, y_):
        return (x_ * NZC + (z_ // 2) * 2 + c_, y_ * 2 + z_ % 2)

    here_other = dev(x, z, 1 - c, y)

    def zc_dev(b):
        return dev(x, (b // 2) * 2 + zl, b % 2, y)

    barrier = pltpu.get_barrier_semaphore()
    greeted = [zc_dev((blk + d) % NZC) for d in range(1, NZC)]
    greeted += [dev(x, (z + 1) % NZ, c, y), dev(x, (z + NZ - 1) % NZ, c, y)]
    for dy in range(1, NY):
        greeted.append(dev(x, z, c, (y + dy) % NY))
        greeted.append(dev(x, z, 1 - c, (y + dy) % NY))
        greeted.append(dev(x, zh * 2 + 1 - zl, c, (y + dy) % NY))
    for dx in range(1, NX):
        greeted.append(dev((x + dx) % NX, z, c, y))
    for there in greeted:
        pl.semaphore_signal(barrier, inc=1, device_id=there, device_id_type=MESH)

    def copy(src, dst, ssem, rsem, where):
        return pltpu.make_async_remote_copy(
            src_ref=src, dst_ref=dst, send_sem=ssem, recv_sem=rsem, device_id=where, device_id_type=MESH
        )

    def send(src, dst, ssem, rsem, where):
        copy(src, dst, ssem, rsem, where).start()

    def arrived(dst, rsem):
        copy(dst, dst, rsem, rsem, here_other).wait_recv()

    def departed(src, ssem):
        copy(src, src, ssem, ssem, here_other).wait_send()

    def column(b):
        return pl.ds(pl.multiple_of(b * ROWS, ROWS), ROWS)

    turned = x_ref[...].T
    for p in range(2):
        for g in range(4):
            Z[zl, pl.ds(BASE[p] + g * PART[p], PART[p]), column(blk)] = turned[
                g * OUT + OFF[p] : g * OUT + OFF[p] + PART[p]
            ]
    partial = jnp.sum(nt(split_rows(w_ref[...].reshape(1, COLS)), x_ref[...]), axis=0, keepdims=True)
    Ls[...] = jnp.broadcast_to(partial, (8, ROWS))
    order = lax.broadcasted_iota(I32, (SKIP, smp_ref.shape[0]), 1)
    rank = lax.broadcasted_iota(I32, (SKIP, smp_ref.shape[0]), 0)
    below = jnp.where(smp_ref[...].reshape(1, -1) - order <= rank, 1.0, 0.0).astype(F32)
    skipped = jnp.sum(below, axis=1, keepdims=True)
    Ix[x, blk] = skipped + lax.broadcasted_iota(I32, (SKIP, 128), 0).astype(F32)

    pl.semaphore_wait(barrier, len(greeted))

    for d in range(1, 8):
        send(Ls, Lr.at[d - 1], ls.at[0], lr.at[0], (row, (feat + d) % 8))
    for d in range(1, NZC):
        mine = Ix.at[x, blk]
        send(mine, mine, ia_s.at[0], ia_r.at[0], zc_dev((blk + d) % NZC))

    def chunk(zsrc, core, p, j):
        b = (zsrc // 2) * 2 + core
        return Z.at[zsrc % 2, pl.ds(BASE[p] + 2 * j * PART[p], 2 * PART[p]), column(b)]

    def to_ring(p, i, step, j, zsrc):
        ref = chunk(zsrc, c, p, j)
        there = dev(x, (z + (1 - 2 * i)) % NZ, c, y)
        send(ref, ref, zs.at[p], zr.at[p, i, step, j], there)

    def gram_rows(p, core):
        start = pl.multiple_of(BASE[p] + (2 * h + core) * PART[p], 32)
        return pl.ds(start, PART[p])

    def kept(p):
        return pl.ds(OFF[p], PART[p])

    def y_copy(p, way, core, zsrc_hi):
        dy = (1, 3)[way]
        b = zsrc_hi * 2 + c
        return copy(
            Z.at[q, gram_rows(p, core), column(b)],
            Y.at[dy - 1, kept(p), column(b)],
            ys.at[p],
            yr.at[p, way, jnp.where(c == way, zsrc_hi, 4)],
            dev(x, z, core, (y + dy) % NY),
        )

    def to_y(p, zsrc, j):
        wanted = zsrc % 2 == q
        if j is not None:
            wanted = wanted & (h == j)

        @pl.when(wanted)
        def _():
            for way in range(2):
                for core in range(2):
                    y_copy(p, way, core, zsrc // 2).start()

    sg = 1 - 2 * h
    pieces = [
        (jnp.where(q == zl, z + a, z + b) + NZ) % NZ
        for a, b in ((0, -sg), (-2 * sg, sg), (2 * sg, -3 * sg), (4, 3 * sg))
    ]

    def y_forward(p, k):
        for way in range(2):
            b = (pieces[k] // 2) * 2 + way
            slot = 2 * way
            ref = Y.at[slot, kept(p), column(b)]
            arrived(ref, yr.at[p, way, pieces[k] // 2])
            there = dev(x, z, c, (y + (1, 3)[way]) % NY)
            send(ref, Y.at[1, kept(p), column(b)], yf.at[p], y2.at[p], there)

    def ring_start(p):
        for jj in range(2):
            for i in range(2):
                to_ring(p, i, 0, jj if i == 0 else 1 - jj, z)
        own = Z.at[zl, pl.ds(BASE[p], 4 * PART[p]), column(blk)]
        send(own, own, cs.at[p], cr.at[p], here_other)
        to_y(p, z, None)

    def ring_event(p, step, jj):
        for i in range(2):
            j = jj if i == 0 else 1 - jj
            zsrc = (z + NZ - (1 - 2 * i) * step) % NZ
            ref = chunk(zsrc, c, p, j)
            arrived(ref, zr.at[p, i, step - 1, j])
            if step < 3 or (step == 3 and jj == 0):
                to_ring(p, i, step, j, zsrc)
            send(ref, ref, cs.at[p], cr.at[p], here_other)
            to_y(p, zsrc, j)

    def sibling_arrived(p):
        arrived(Z.at[zl, pl.ds(BASE[p], 4 * PART[p]), :], cr.at[p])

    ring_start(0)

    ring_event(0, 1, 0)
    ring_event(0, 1, 1)

    logits = Ls[0:1, :]
    arrived(Lr, lr.at[0])
    for d in range(1, 8):
        logits = logits + Lr[d - 1, 0:1, :]
    prob = 1.0 / (1.0 + jnp.exp(-logits))
    var = prob * (1.0 - prob)
    resid = prob - lab_ref[...].reshape(1, ROWS).astype(F32)
    scale = (2 * sgn_ref[...].reshape(1, ROWS) - 1).astype(F32) * jnp.sqrt(var)
    rid8 = lax.broadcasted_iota(I32, (8, ROWS), 0)
    St[blk] = jnp.where(rid8 == 0, var, jnp.where(rid8 == 1, resid, scale))
    for d in range(1, NZC):
        send(St.at[blk], St.at[blk], ss.at[0], sr.at[0], zc_dev((blk + d) % NZC))

    arrived(Ix.at[x, 0:7], ia_r.at[0])
    for dx in range(1, NX):
        send(Ix.at[x], Ix.at[x], ib_s.at[0], ib_r.at[0], dev((x + dx) % NX, z, c, y))

    ring_event(0, 2, 0)
    y_forward(0, 0)

    arrived(Ix.at[0:3], ib_r.at[0])
    index = jnp.concatenate([Ix[u, 2 * v + c] for u in range(NX) for v in range(4)], axis=0).astype(I32)
    lane = lax.broadcasted_iota(I32, index.shape, 1)
    place = lax.broadcasted_iota(I32, index.shape, 0) // SKIP
    block = (place // 4) * NZC + (place % 4) * 2 + c

    def parity(u):
        u = u ^ (u >> 8)
        u = u ^ (u >> 4)
        u = u ^ (u >> 2)
        u = u ^ (u >> 1)
        return u & 1

    low = parity(index & lane)
    high = low ^ ((index >> 7) & 1)
    for b in range(NZC):
        flip = parity(block & (x * NZC + b))
        for part, bits in enumerate((low, high)):
            La[0:TABLE, b * ROWS + part * 128 : b * ROWS + part * 128 + 128] = (1 - 2 * (bits ^ flip)).astype(F32).astype(BF16)

    ring_event(0, 2, 1)
    ring_event(0, 3, 0)
    y_forward(0, 1)
    ring_event(0, 3, 1)
    ring_start(1)

    arrived(St.at[0:7], sr.at[0])
    weight = jnp.concatenate([St[b, 0:1, :] for b in range(NZC)], axis=1)
    resids = jnp.concatenate([St[b, 1:2, :] for b in range(NZC)], axis=1)
    scales = jnp.concatenate([St[b, 2:3, :] for b in range(NZC)], axis=1)

    def region(p, shape, half=None):
        start, height = (0, OFF[p]) if shape == 0 else (OFF[p], PART[p])
        width = (BASE[p], 4 * PART[p]) if shape == 0 else (0, BASE[p] + 4 * PART[p])
        if half is not None:
            start, height = start + half * (height // 2), height // 2
        return (pl.ds(start, height), pl.ds(*width))

    def features(p):
        return pl.ds(BASE[p], 4 * PART[p])

    def left(dy, start, height):
        if dy == 0:
            return La.at[HEAD + start : HEAD + start + height]
        return Lb.at[dy - 1, start : start + height]

    def prepare(dy, p):
        rows = Z[q, gram_rows(p, c), :] if dy == 0 else Y[dy - 1, kept(p), :]
        scaled = rows.astype(F32) * weight
        high = scaled.astype(BF16)
        left(dy, 2 * OFF[p], PART[p])[...] = high
        left(dy, 2 * OFF[p] + PART[p], PART[p])[...] = (scaled - high.astype(F32)).astype(BF16)

    def product(dy, p):
        both = nt(left(dy, 0, 2 * PART[0])[...], Z[zl, features(p), :])
        Gm[dy, kept(0), features(p)] = both[: PART[0]] + both[PART[0] :]

    def product_rest():
        height = 2 * PART[0]
        rows = jnp.concatenate([left(dy, 0, height)[...] for dy in range(1, NY)], axis=0)
        all_rows = nt(rows, Z[zl, features(1), :])
        for dy in range(1, NY):
            one = all_rows[(dy - 1) * height : dy * height]
            Gm[dy, kept(0), features(1)] = one[: PART[0]] + one[PART[0] :]

    def product_last():
        height = 2 * PART[1]
        rows = jnp.concatenate([left(dy, 2 * OFF[1], height)[...] for dy in range(NY)], axis=0)
        for p in range(2):
            all_rows = nt(rows, Z[zl, features(p), :])
            for dy in range(NY):
                one = all_rows[dy * height : (dy + 1) * height]
                Gm[dy, kept(1), features(p)] = one[: PART[1]] + one[PART[1] :]

    def product_own(p):
        all_rows = nt(La[0 : HEAD + 2 * PART[0]], Z[zl, features(p), :])
        Cs[:, features(p)] = all_rows[:TABLE].astype(BF16)
        for dx in (2, 1, 3):
            there = (x + dx) % NX
            send(
                Cs.at[plane_rows(there), features(p)], Cx.at[dx - 1, :, features(p)],
                cx_s.at[p], cx_r.at[p], dev(there, z, c, y),
            )
        Gs[:, features(p)] = jnp.broadcast_to(
            jnp.sum(all_rows[TABLE:HEAD], axis=0, keepdims=True), (8, 4 * PART[p])
        )
        Gm[0, kept(0), features(p)] = all_rows[HEAD : HEAD + PART[0]] + all_rows[HEAD + PART[0] :]

    def corrected(dx, where):
        dy = (y - x - dx + 2 * NY) % NY
        return Gm[(dy,) + where] - nn(Cy[dy, where[0], :], Cg[:, where[1]]) * (1.0 / TOTAL)

    def finish_far(p, shape):
        whole = region(p, shape)
        Gb[(1,) + whole] = corrected(2, whole).astype(BF16)
        for half in range(2):
            where = region(p, shape, half)
            there = dev((x + 1 + 2 * half) % NX, z, c, y)
            send(Gb.at[(1,) + where], Gf.at[where], f_s.at[p, shape], f_r.at[p, shape], there)
        Gown[whole] = corrected(0, whole)

    def finish_near(p, shape):
        whole = region(p, shape)
        arrived(Gf.at[whole], f_r.at[p, shape])
        for half in range(2):
            dx = 1 + 2 * half
            added, plain = region(p, shape, half), region(p, shape, 1 - half)
            Gb[(2 * half,) + added] = (corrected(dx, added) + Gf[added].astype(F32)).astype(BF16)
            Gb[(2 * half,) + plain] = corrected(dx, plain).astype(BF16)
            send(
                Gb.at[(2 * half,) + whole], Gr.at[(half,) + whole],
                g_s.at[p, shape], g_r.at[p, shape], dev((x + dx) % NX, z, c, y),
            )

    def y_arrived(p, dy):
        if dy == 2:
            arrived(Y.at[1, kept(p), :], y2.at[p])
        else:
            arrived(Y.at[dy - 1, kept(p), 0 : DEPTH // 2], yr.at[p, dy // 2, 4])

    def half_rows(core):
        return pl.ds(pl.multiple_of(core * 4 * SKIP, 4 * SKIP), 4 * SKIP)

    def plane_rows(u):
        return pl.ds(pl.multiple_of(u * 4 * SKIP, 4 * SKIP), 4 * SKIP)

    def skipped_sum(p):
        total = Cs[plane_rows(x), features(p)].astype(F32)
        arrived(Cx.at[:, :, features(p)], cx_r.at[p])
        for dx in range(1, NX):
            total = total + Cx[dx - 1, :, features(p)].astype(F32)
        mine = Cg.at[half_rows(c), features(p)]
        mine[...] = total.astype(BF16)
        send(mine, mine, cg_s.at[p], cg_r.at[p], here_other)

    def c_copy(p, dy, far):
        there = dev(x, zh * 2 + (1 - zl if far else zl), c, (y + dy) % NY)
        return copy(
            CT.at[gram_rows(p, c), :], Cy.at[dy, kept(p), :], cy_s.at[p, far], cy_r.at[p, dy], there
        )

    c_targets = [(dy, far) for dy in (1, 3, 2, 0) for far in range(2) if dy or far]

    def skipped_spread(p):
        arrived(Cg.at[half_rows(1 - c), features(p)], cg_r.at[p])

        @pl.when(q == zl)
        def _():
            CT[features(p), :] = Cg[:, features(p)].T
            for dy, far in c_targets:
                c_copy(p, dy, far).start()
            Cy[0, kept(p), :] = CT[gram_rows(p, c), :]

    def skipped_arrived(p, dy):
        if dy:
            arrived(Cy.at[dy, kept(p), :], cy_r.at[p, dy])
        else:

            @pl.when(q != zl)
            def _():
                arrived(Cy.at[dy, kept(p), :], cy_r.at[p, dy])

    La[0:TABLE] = (La[0:TABLE].astype(F32) * scales).astype(BF16)
    La[TABLE:HEAD] = split_rows(resids)
    ring_event(0, 4, 0)
    y_forward(0, 2)
    sibling_arrived(0)
    prepare(0, 0)
    product_own(0)
    ring_event(1, 1, 0)
    ring_event(1, 1, 1)
    ring_event(1, 2, 0)
    y_forward(0, 3)
    ring_event(1, 2, 1)
    skipped_sum(0)
    ring_event(1, 3, 0)
    y_forward(1, 0)
    y_arrived(0, 1)
    prepare(1, 0)
    product(1, 0)
    ring_event(1, 3, 1)
    skipped_spread(0)
    y_arrived(0, 3)
    prepare(3, 0)
    product(3, 0)
    ring_event(1, 4, 0)
    y_forward(1, 1)
    sibling_arrived(1)
    product_own(1)
    for dx in range(1, NX):
        send(Gs, Grr.at[dx - 1], d_s.at[0], d_r.at[0], dev((x + dx) % NX, z, c, y))
    y_arrived(0, 2)
    prepare(2, 0)
    product(2, 0)
    for dy in range(NY):
        skipped_arrived(0, dy)
    finish_far(0, 1)
    y_forward(1, 2)
    y_forward(1, 3)
    product_rest()
    skipped_sum(1)
    prepare(0, 1)
    y_arrived(1, 1)
    prepare(1, 1)
    skipped_spread(1)
    finish_far(1, 0)
    finish_near(0, 1)
    for dy in (3, 2):
        y_arrived(1, dy)
        prepare(dy, 1)
    product_last()
    for dy in range(NY):
        skipped_arrived(1, dy)
    finish_far(1, 1)
    finish_near(1, 0)

    def natural(v):
        cuts = []
        for g in range(4):
            for p in range(2):
                start = BASE[p] + g * PART[p]
                cuts.append(v[:, start : start + PART[p]])
        return jnp.concatenate(cuts, axis=1)

    departed(Lr, ls.at[0])
    departed(Ix.at[x, 0:7], ia_s.at[0])
    departed(Ix.at[0:3], ib_s.at[0])
    departed(St.at[0:7], ss.at[0])
    for p in range(2):
        departed(Z.at[0, features(p), 0 : 7 * ROWS], zs.at[p])
        departed(Z.at[0, features(p), :], cs.at[p])
        departed(Y.at[0:2, kept(p), :], ys.at[p])
        departed(Y.at[0, kept(p), :], yf.at[p])
        departed(Cx.at[:, :, features(p)], cx_s.at[p])
        departed(Cg.at[half_rows(c), features(p)], cg_s.at[p])

    @pl.when(q == zl)
    def _():
        for p in range(2):
            departed(Cy.at[0:3, kept(p), :], cy_s.at[p, 0])
            departed(Cy.at[:, kept(p), :], cy_s.at[p, 1])

    total = Gs[...]
    arrived(Grr, d_r.at[0])
    for dx in range(1, NX):
        total = total + Grr[dx - 1]
    grad_ref[...] = (natural(total)[0:1, :] * (TOTAL ** -0.5)).reshape(COLS)
    departed(Grr, d_s.at[0])

    finish_near(1, 1)
    regions = [(0, 1), (1, 0), (1, 1)]
    for p, shape in regions:
        arrived(Gr.at[(slice(None),) + region(p, shape)], g_r.at[p, shape])
    total = Gown[...] + Gr[0].astype(F32) + Gr[1].astype(F32)
    gram_ref[...] = natural(total) * (SKETCH ** -0.5)
    for p, shape in regions:
        departed(Gb.at[(1,) + region(p, shape)], f_s.at[p, shape])
        departed(Gr.at[(slice(None),) + region(p, shape)], g_s.at[p, shape])


def shards(features, weights, labels, sign_bits, sample_rows):
    vmem = pl.BlockSpec(memory_space=pltpu.VMEM)
    dma = pltpu.SemaphoreType.DMA
    scratch = [
        pltpu.VMEM((2, COLS, DEPTH), BF16),
        pltpu.VMEM((3, OUT, DEPTH), BF16),
        pltpu.VMEM((8, ROWS), F32),
        pltpu.VMEM((7, 8, ROWS), F32),
        pltpu.VMEM((NZC, 8, ROWS), F32),
        pltpu.VMEM((NX, NZC, SKIP, 128), F32),
        pltpu.VMEM((HEAD + 2 * OUT, DEPTH), BF16),
        pltpu.VMEM((3, 2 * OUT, DEPTH), BF16),
        pltpu.VMEM((NX * 4 * SKIP, COLS), BF16),
        pltpu.VMEM((3, 4 * SKIP, COLS), BF16),
        pltpu.VMEM((NZC * SKIP, COLS), BF16),
        pltpu.VMEM((COLS, NZC * SKIP), BF16),
        pltpu.VMEM((NY, OUT, NZC * SKIP), BF16),
        pltpu.VMEM((NY, OUT, COLS), F32),
        pltpu.VMEM((3, OUT, COLS), BF16),
        pltpu.VMEM((OUT, COLS), F32),
        pltpu.VMEM((OUT, COLS), BF16),
        pltpu.VMEM((2, OUT, COLS), BF16),
        pltpu.VMEM((8, COLS), F32),
        pltpu.VMEM((3, 8, COLS), F32),
        dma((2,)), dma((2, 2, 4, 2)),
        dma((2,)), dma((2,)),
        dma((2,)), dma((2, 2, 5)), dma((2,)), dma((2,)),
        dma((1,)), dma((1,)),
        dma((1,)), dma((1,)),
        dma((1,)), dma((1,)),
        dma((1,)), dma((1,)),
        dma((2,)), dma((2,)),
        dma((2,)), dma((2,)),
        dma((2, 4)), dma((2, 2)),
        dma((2, 2)), dma((2, 2)),
        dma((2, 2)), dma((2, 2)),
        dma((1,)), dma((1,)),
    ]
    gram, gradient = pl.pallas_call(
        kernel,
        out_shape=(
            jax.ShapeDtypeStruct((OUT, COLS), F32),
            jax.ShapeDtypeStruct((COLS,), F32),
        ),
        in_specs=[vmem] * 5,
        out_specs=(vmem, vmem),
        scratch_shapes=scratch,
        compiler_params=pltpu.CompilerParams(
            collective_id=0, has_side_effects=True, vmem_limit_bytes=56 * 2**20
        ),
        name="newton_sketch",
    )(
        features, weights, labels, sign_bits, sample_rows
    )
    return gram, gradient


def solution(mesh):
    placed = (P("row", "feat"), P("feat"), P("row"), P("row"), P("row"))
    return jax.shard_map(
        shards, mesh=mesh, in_specs=placed, out_specs=(P("row", "feat"), P("feat")), check_vma=False
    )
```
